32 devices in a mesh: blk: 16 (over z, y, x), mp: 2 (over core).
Axes of the slice: x: 2, y: 2, z: 4, core: 2. Of those that a mesh axis runs over, the one named last changes fastest.
Arguments:
- tokens: bfloat16 [4096, 1536], P('blk'), may hold values from -6 to 6
- cotangent: bfloat16 [4096, 1536], P('blk'), may hold values from -6 to 6
- norm_gain: bfloat16 [1536], replicated, may hold values from 0.5 to 1.5
- w_query: bfloat16 [1536, 1536], P('blk', 'mp'), may hold values from -0.15625 to 0.15625
- b_query: bfloat16 [1536], P('mp'), may hold values from -3 to 3
- w_key: bfloat16 [1536, 256], P('blk', 'mp'), may hold values from -0.15625 to 0.15625
- b_key: bfloat16 [256], P('mp'), may hold values from -3 to 3
- w_value: bfloat16 [1536, 256], P('blk', 'mp'), may hold values from -0.15625 to 0.15625
- b_value: bfloat16 [256], P('mp'), may hold values from -3 to 3
- w_out: bfloat16 [1536, 1536], P('mp', 'blk'), may hold values from -2 to 2
- ffn_gain: bfloat16 [1536], replicated, may hold values from 0.5 to 1.5
- w_gate: bfloat16 [1536, 8960], P('blk', 'mp'), may hold values from -0.15625 to 0.15625
- w_up: bfloat16 [1536, 8960], P('blk', 'mp'), may hold values from -0.15625 to 0.15625
- w_down: bfloat16 [8960, 1536], P('mp', 'blk'), may hold values from -0.125 to 0.125
- unit_seq: int32 [4], replicated, may hold values from 0 to 2, as said below
- block_map: int32 [16], replicated, may hold values from 0 to 15, as said below
Outputs:
- mixed: bfloat16 [4096, 1536], P('blk')
- g_tokens: float32 [4096, 1536], P('blk')
- g_norm_gain: float32 [1536], replicated
- g_query: float32 [1536, 1536], P('blk', 'mp')
- g_query_bias: float32 [1536], P('mp')
- g_key: float32 [1536, 256], P('blk', 'mp')
- g_key_bias: float32 [256], P('mp')
- g_value: float32 [1536, 256], P('blk', 'mp')
- g_value_bias: float32 [256], P('mp')
- g_out: float32 [1536, 1536], P('mp', 'blk')
- g_ffn_gain: float32 [1536], replicated
- g_gate: float32 [1536, 8960], P('blk', 'mp')
- g_up: float32 [1536, 8960], P('blk', 'mp')
- g_down: float32 [8960, 1536], P('mp', 'blk')
The draws below stay inside these ranges and needn't reach their ends.
Inputs may be any that keep to these rules, and one draw needn't show every extreme that they name: `unit_seq`: starts at 0 and rises by 0 or 1 from unit to unit; one sequence, at a place drawn from the seed, covers exactly 2 consecutive units, every other sequence 1 or 4 units. `block_map`: A permutation of the logical token blocks; index 0 of blk holds the block with the first token of the sequence of 2 units and the last index the block with its last token.
All inputs are finite; a program needn't handle non-finite values.
Results may differ from the reference program's by a relative error of at most 0.039.
Values may be sent and summed in bfloat16 or wider, within the bound.
No kernel may reach another device: no remote copies, remote signals or barrier semaphores. Data moves between devices by JAX's collectives and lax.ppermute only.
A program may use at most 320 MiB of HBM per device.

```python
import math
import jax
import jax.numpy as jnp
from jax import lax

D = 1536
FF = 8960
QH = 12
KVH = 2
HD = 128
TOK_DEV = 256
SEG = 1024
TOKENS = 4096
UNITS = 4
BLOCKS = 16


def unit_layout(key):
    long_key, coin_key = jax.random.split(key)
    offset = jax.random.randint(long_key, (), 0, UNITS // 2 + 1).astype(jnp.int32)
    place = jnp.arange(UNITS, dtype=jnp.int32)
    inside = (place >= offset) & (place < offset + UNITS // 2)
    quartet = place - place % 4
    whole = ((quartet + 4 <= offset) | (quartet >= offset + UNITS // 2)) & (quartet + 4 <= UNITS)
    coins = jax.random.randint(coin_key, (UNITS // 4 + 1,), 0, 2)
    joined = whole & (coins[place // 4] == 1)
    outside_begin = (place % 4 == 0) | jnp.logical_not(joined)
    begins = jnp.where(inside, place == offset, outside_begin)
    seq = jnp.cumsum(begins.astype(jnp.int32)) - 1
    return (seq.astype(jnp.int32), offset)


def draw_unit_seq(key, part):
    seq, offset = unit_layout(key)
    return seq


def draw_block_map(key, part):
    seq, offset = unit_layout(key)
    key = jax.random.fold_in(key, 7)
    scores = jax.random.permutation(key, BLOCKS).astype(jnp.int32)
    place = jnp.arange(BLOCKS, dtype=jnp.int32)
    first = offset * SEG // TOK_DEV
    last = ((offset + UNITS // 2) * SEG - 1) // TOK_DEV
    scores = jnp.where(place == first, -1, scores)
    scores = jnp.where(place == last, BLOCKS, scores)
    return jnp.argsort(scores, stable=True).astype(jnp.int32)


def block_levels(key, shape, pieces, low, high):
    level, own = 1.0, jax.random.fold_in(key, 6)
    for axis_at, shards_of in pieces:
        draws = jnp.exp(jax.random.uniform(jax.random.fold_in(own, axis_at), (shards_of,), jnp.float32, low / len(pieces), high / len(pieces)))
        level = level * jnp.repeat(draws, shape[axis_at] // shards_of).reshape([-1 if axis == axis_at else 1 for axis in range(len(shape))])
    return level


def scatter_about(rng, dims, scale, limit, shards=(), kind=jnp.bfloat16):
    values = scale * jax.random.normal(rng, dims, jnp.float32)
    if shards:
        values = values * block_levels(rng, dims, shards, -0.22, 0.18)
    return jnp.clip(values, -limit, limit).astype(kind)


def setup_inputs(seed: int = 0) -> dict:
    streams_of = jax.random.split(jax.random.key(seed), 17)
    tokens = scatter_about(streams_of[0], (TOKENS, D), 1.0, 6.0, ((0, 16),))
    cotangent = scatter_about(streams_of[1], (TOKENS, D), 1.0, 6.0, ((0, 16),))
    norm_gain = jnp.clip(1.0 + 0.1 * jax.random.normal(streams_of[2], (D,), jnp.float32), 0.5, 1.5).astype(jnp.bfloat16)
    w_query = scatter_about(streams_of[3], (D, QH * HD), D ** -0.5, 0.15625, ((0, 16), (1, 2)))
    b_query = scatter_about(streams_of[4], (QH * HD,), 0.5, 3.0, ((0, 2),))
    w_key = scatter_about(streams_of[5], (D, KVH * HD), D ** -0.5, 0.15625, ((0, 16), (1, 2)))
    b_key = scatter_about(streams_of[6], (KVH * HD,), 0.5, 3.0, ((0, 2),))
    w_value = scatter_about(streams_of[7], (D, KVH * HD), D ** -0.5, 0.15625, ((0, 16), (1, 2)))
    b_value = scatter_about(streams_of[8], (KVH * HD,), 0.5, 3.0, ((0, 2),))
    w_out = scatter_about(streams_of[9], (QH * HD, D), 8 ** -0.5, 2.0, ((0, 2), (1, 16)))
    ffn_gain = jnp.clip(1.0 + 0.1 * jax.random.normal(streams_of[10], (D,), jnp.float32), 0.5, 1.5).astype(jnp.bfloat16)
    w_gate = scatter_about(streams_of[11], (D, FF), D ** -0.5, 0.15625, ((0, 16), (1, 2)))
    w_up = scatter_about(streams_of[12], (D, FF), D ** -0.5, 0.15625, ((0, 16), (1, 2)))
    w_down = scatter_about(streams_of[13], (FF, D), (FF // 4) ** -0.5, 0.125, ((0, 2), (1, 16)))
    unit_seq = draw_unit_seq(jax.random.fold_in(streams_of[16], 71), 0)
    block_map = draw_block_map(jax.random.fold_in(streams_of[16], 71), 0)
    return dict(tokens=tokens, cotangent=cotangent, norm_gain=norm_gain, w_query=w_query, b_query=b_query, w_key=w_key, b_key=b_key, w_value=w_value, b_value=b_value, w_out=w_out, ffn_gain=ffn_gain, w_gate=w_gate, w_up=w_up, w_down=w_down, unit_seq=unit_seq, block_map=block_map)


precise = lax.Precision.HIGHEST
epsilon = 1e-06

@jax.custom_vjp
def low(v):
    return lax.optimization_barrier(v.astype(jnp.bfloat16)).astype(jnp.float32)

@jax.custom_vjp
def low_back(v):
    return v

def low_keep(v):
    return (low(v), None)

def low_pass(kept, grad):
    return (grad,)

def back_keep(v):
    return (v, None)

def back_low(kept, grad):
    return (low(grad),)
low.defvjp(low_keep, low_pass)
low_back.defvjp(back_keep, back_low)

def matmul(left, right):
    return jnp.dot(left, right, precision=precise, preferred_element_type=jnp.float32)

def rms_scale(value, gain):
    return value * lax.rsqrt(lax.optimization_barrier(jnp.mean(value * value, axis=-1, keepdims=True)) + epsilon) * gain

def rotate(value, cosine, sine):
    half = value.shape[-1] // 2
    first = value[..., :half]
    second = value[..., half:]
    return jnp.concatenate([first * cosine - second * sine, second * cosine + first * sine], axis=-1)

def token_tables(unit_seq, block_map):
    place = jnp.arange(TOKENS, dtype=jnp.int32)
    logical = (block_map[place // TOK_DEV] * TOK_DEV + place % TOK_DEV).astype(jnp.int32)
    units = jnp.arange(UNITS, dtype=jnp.int32)
    previous = jnp.concatenate([jnp.full((1,), -1, jnp.int32), unit_seq[:-1]])
    first = lax.cummax(jnp.where(unit_seq != previous, units, 0), axis=0)
    unit = logical // SEG
    return (unit_seq[unit], logical, logical - first[unit] * SEG)

def rope_tables(position):
    freq = jnp.power(10000.0, -(jnp.arange(HD // 2, dtype=jnp.float32) * (2.0 / HD)))
    angle = position.astype(jnp.float32)[:, None] * freq[None, :]
    return (jnp.cos(angle)[:, None, :], jnp.sin(angle)[:, None, :])

def attention(query, keys, values, seq, logical):
    width = math.gcd(TOKENS, 512)
    count = TOKENS // width
    scale = HD ** (-0.5)
    grouped = query.reshape(count, width, KVH, QH // KVH, HD)

    def one_block(inputs):
        block, block_seq, block_log = inputs
        scores = low_back(jnp.einsum('qgjd,kgd->gjqk', block, keys, precision=precise) * scale)
        mask = (block_seq[:, None] == seq[None, :]) & (logical[None, :] <= block_log[:, None])
        scores = jnp.where(mask[None, None], scores, -1e+30)
        top = lax.optimization_barrier(jnp.max(scores, axis=-1, keepdims=True))
        weights = jnp.exp(scores - top)
        probs = weights / lax.optimization_barrier(jnp.sum(weights, axis=-1, keepdims=True))
        return jnp.einsum('gjqk,kgd->qgjd', low(probs), values, precision=precise)
    result = lax.map(jax.checkpoint(one_block), (grouped, seq.reshape(count, width), logical.reshape(count, width)))
    return result.reshape(TOKENS, QH * HD)

def reference(tokens, cotangent, norm_gain, w_query, b_query, w_key, b_key, w_value, b_value, w_out, ffn_gain, w_gate, w_up, w_down, unit_seq, block_map):
    seq, logical, position = token_tables(unit_seq, block_map)
    cosine, sine = rope_tables(position)

    def forward(inputs, gain1, query_w, query_b, key_w, key_b, value_w, value_b, out_w, gain2, gate_w, up_w, down_w):
        normed = low(rms_scale(inputs, gain1))
        qlin = low_back(matmul(normed, query_w) + query_b).reshape(TOKENS, QH, HD)
        klin = low_back(matmul(normed, key_w) + key_b).reshape(TOKENS, KVH, HD)
        values = low(low_back(matmul(normed, value_w) + value_b)).reshape(TOKENS, KVH, HD)
        query = low(rotate(qlin, cosine, sine))
        keys = low(rotate(klin, cosine, sine))
        attended = low(low_back(attention(query, keys, values, seq, logical)))
        middle = inputs + low_back(matmul(attended, out_w))
        normed2 = low(rms_scale(middle, gain2))
        gate = low_back(matmul(normed2, gate_w))
        up = low_back(matmul(normed2, up_w))
        hidden = low(jax.nn.silu(gate) * up)
        return middle + low_back(matmul(hidden, down_w))
    floats = [a.astype(jnp.float32) for a in (tokens, norm_gain, w_query, b_query, w_key, b_key, w_value, b_value, w_out, ffn_gain, w_gate, w_up, w_down)]
    output, pull = jax.vjp(forward, *floats)
    grads = pull(cotangent.astype(jnp.float32))
    return (output.astype(jnp.bfloat16), grads[0], grads[1], grads[2], grads[3], grads[4], grads[5], grads[6], grads[7], grads[8], grads[9], grads[10], grads[11], grads[12])
```

```python
import functools

import jax
import jax.numpy as jnp
from jax import lax
from jax.experimental import pallas as pl
from jax.experimental.pallas import tpu as pltpu
from jax.sharding import Mesh
from jax.sharding import PartitionSpec as P

HD = 128
SEG = 1024
LOG2E = 1.4426950408889634
BIG = -1e30
BF = jnp.bfloat16
F32 = jnp.float32

epsilon = 1e-06


def bit_axis(bit):
    return ("x", "y", "a")[bit] if bit < 3 else "h", 1 if bit < 3 else 1 << (bit - 3)


def flip(value, bit):
    axis, mask = bit_axis(bit)
    return lax.ppermute(value, axis, [(i, i ^ mask) for i in range(lax.axis_size(axis))])


def mine(bit):
    axis, mask = bit_axis(bit)
    return (lax.axis_index(axis) // mask) % 2


def swap_mp(value):
    return lax.ppermute(value, "mp", [(0, 1), (1, 0)])


def halves(value, which):
    return lax.dynamic_index_in_dim(value, which, 0, keepdims=False)


def gather_bits(value, order):
    rows, width = value.shape
    have = []
    for bit in order:
        at = sum(1 for b in have if b > bit)
        other = flip(value, bit)
        value = jnp.where(
            mine(bit) == 0, jnp.stack([value, other], at), jnp.stack([other, value], at)
        )
        have.append(bit)
    return value.reshape(-1, width)


def scatter_bits(value, order, blocks):
    width = value.shape[-1]
    have = sorted(order, reverse=True)
    value = value.reshape((2,) * len(order) + (-1, width))
    for bit in order:
        at = have.index(bit)
        me = mine(bit)
        keep = lax.dynamic_index_in_dim(value, me, at, keepdims=False)
        send = lax.dynamic_index_in_dim(value, 1 - me, at, keepdims=False)
        value = (keep.astype(F32) + flip(send, bit).astype(F32)).astype(BF)
        have.remove(bit)
    return value


CUBE = ((0, 1, 2), (1, 2, 0), (2, 0, 1))


def cube_parts(rows):
    units = rows // 8
    sizes = [(units + 2 - i) // 3 * 8 for i in range(3)]
    return sizes


def cube_gather(value):
    parts, at = [], 0
    for size in cube_parts(value.shape[0]):
        parts.append(value[at : at + size])
        at += size
    for step in range(3):
        parts = [
            jnp.concatenate([part, flip(part, order[step])], 0) for part, order in zip(parts, CUBE)
        ]
    return jnp.concatenate(parts, 0)


def cube_scatter(value, rows):
    parts, at = [], 0
    for size in cube_parts(rows):
        parts.append(value[at : at + 8 * size])
        at += 8 * size
    for step in range(3):
        new = []
        for part, order in zip(parts, CUBE):
            half = part.shape[0] // 2
            other = flip(part[half:], order[2 - step])
            total = part[:half].astype(F32) + other.astype(F32)
            new.append(total if step == 2 else total.astype(BF))
        parts = new
    return jnp.concatenate(parts, 0)


def slot_gather(value, order):
    for bit in order:
        value = jnp.concatenate([value, flip(value, bit)], 0)
    return value


def slot_scatter(value, order):
    for bit in order:
        half = value.shape[0] // 2
        value = value[:half].astype(F32) + flip(value[half:], bit).astype(F32)
        if bit != order[-1]:
            value = value.astype(BF)
    return value


def slot_places(order):
    places = [0]
    for bit in order:
        places = places + [p ^ (1 << bit) for p in places]
    return places


def rotate(value, cosine, sine):
    half = value.shape[-1] // 2
    first = value[..., :half]
    second = value[..., half:]
    return jnp.concatenate(
        [first * cosine - second * sine, second * cosine + first * sine], axis=-1
    )


def rope_tables(position):
    freq = jnp.power(10000.0, -(jnp.arange(HD // 2, dtype=F32) * (2.0 / HD)))
    angle = position.astype(F32)[:, None] * freq[None, :]
    return (jnp.cos(angle)[:, None, :], jnp.sin(angle)[:, None, :])


def look(table, index):
    places = jnp.arange(table.shape[0], dtype=jnp.int32)
    return jnp.sum(jnp.where(index[:, None] == places[None, :], table[None, :], 0), axis=1)


def norm_back(grad, value, inverse, gain):
    scaled = grad * gain
    grad_gain = jnp.sum(grad * value * inverse, axis=0)
    mean_term = jnp.mean(scaled * value, axis=-1, keepdims=True)
    grad_value = inverse * scaled - value * (inverse * inverse * inverse) * mean_term
    return (grad_value, grad_gain)


NT = (((1,), (1,)), ((), ()))
TN = (((0,), (0,)), ((), ()))


def dot(left, right, dims=(((1,), (0,)), ((), ()))):
    return lax.dot_general(left, right, dims, preferred_element_type=F32)


def attend_kernel(vis, vat, q_ref, k_ref, v_ref, o_ref, low_ref, lse_ref, acc, top, tot):
    rows, width = q_ref.shape
    heads = width // HD
    factor = HD ** (-0.5) * LOG2E

    def block(place, first):
        key = k_ref[place]
        value = v_ref[vat[place]]
        if first:
            mask = lax.broadcasted_iota(jnp.int32, (rows, rows), 0) >= lax.broadcasted_iota(
                jnp.int32, (rows, rows), 1
            )
        for h in range(heads):
            cols = slice(h * HD, (h + 1) * HD)
            scores = dot(q_ref[:, cols], key, NT) * factor
            if first:
                scores = jnp.where(mask, scores, BIG)
                best = jnp.max(scores, axis=1, keepdims=True)
                weights = jnp.exp2(scores - best)
                tot[h] = jnp.sum(weights, axis=1, keepdims=True)
                acc[:, cols] = dot(weights.astype(BF), value)
            else:
                old = top[h]
                best = jnp.maximum(old, jnp.max(scores, axis=1, keepdims=True))
                weights = jnp.exp2(scores - best)
                scale = jnp.exp2(old - best)
                tot[h] = tot[h] * scale + jnp.sum(weights, axis=1, keepdims=True)
                acc[:, cols] = acc[:, cols] * scale + dot(weights.astype(BF), value)
            top[h] = best

    block(0, True)

    def step(place, carry):
        @pl.when(vis[place] == 1)
        def _():
            block(place, False)

        return carry

    lax.fori_loop(1, k_ref.shape[0], step, 0)
    for h in range(heads):
        cols = slice(h * HD, (h + 1) * HD)
        total = tot[h]
        out = acc[:, cols] / total
        o_ref[:, cols] = out
        low_ref[:, cols] = out.astype(BF)
        lse_ref[:, cols] = jnp.broadcast_to(top[h] + jnp.log(total) * LOG2E, (rows, HD))


def attend(vis, vat, query, keys, values):
    rows, width = query.shape
    heads = width // HD
    smem = pl.BlockSpec(memory_space=pltpu.SMEM)
    vmem = pl.BlockSpec(memory_space=pltpu.VMEM)
    return pl.pallas_call(
        attend_kernel,
        out_shape=(
            jax.ShapeDtypeStruct((rows, width), F32),
            jax.ShapeDtypeStruct((rows, width), BF),
            jax.ShapeDtypeStruct((rows, width), F32),
        ),
        in_specs=[smem, smem, vmem, vmem, vmem],
        out_specs=(vmem, vmem, vmem),
        scratch_shapes=[
            pltpu.VMEM((rows, width), F32),
            pltpu.VMEM((heads, rows, 1), F32),
            pltpu.VMEM((heads, rows, 1), F32),
        ],
        compiler_params=pltpu.CompilerParams(vmem_limit_bytes=40 * 2**20),
        cost_estimate=pl.CostEstimate(
            flops=4 * rows * width * 2048, bytes_accessed=8 * 2**20, transcendentals=rows * 6 * 2048
        ),
    )(vis, vat, query, keys, values)


def attend_back_kernel(
    vis, vat, q_ref, k_ref, v_ref, do_ref, o_ref, lse_ref, dq_ref, dk_ref, dv_ref, delta
):
    rows, width = q_ref.shape
    heads = width // HD
    scale = HD ** (-0.5)
    for h in range(heads):
        cols = slice(h * HD, (h + 1) * HD)
        delta[h] = jnp.sum(do_ref[:, cols].astype(F32) * o_ref[:, cols], axis=1, keepdims=True)
    dk_ref[...] = jnp.zeros_like(dk_ref)
    dv_ref[...] = jnp.zeros_like(dv_ref)

    def block(place, first):
        key = k_ref[place]
        value = v_ref[vat[place]]
        if first:
            mask = lax.broadcasted_iota(jnp.int32, (rows, rows), 0) >= lax.broadcasted_iota(
                jnp.int32, (rows, rows), 1
            )
        dk = jnp.zeros((rows, HD), F32)
        dv = jnp.zeros((rows, HD), F32)
        for h in range(heads):
            cols = slice(h * HD, (h + 1) * HD)
            query = q_ref[:, cols]
            grad = do_ref[:, cols]
            probs = jnp.exp2(
                dot(query, key, NT) * (scale * LOG2E) - lse_ref[:, h * HD : h * HD + 1]
            )
            if first:
                probs = jnp.where(mask, probs, 0.0)
            dv = dv + dot(probs.astype(BF), grad, TN)
            dprobs = dot(grad, value, NT)
            dscores = (probs * (dprobs - delta[h])).astype(BF)
            dk = dk + dot(dscores, query, TN)
            dq = dot(dscores, key) * scale
            if first:
                dq_ref[:, cols] = dq
            else:
                dq_ref[:, cols] = dq_ref[:, cols] + dq
        dk_ref[place] = (dk * scale).astype(BF)
        dv_ref[vat[place]] = dv.astype(BF)

    block(0, True)

    def step(place, carry):
        @pl.when(vis[place] == 1)
        def _():
            block(place, False)

        return carry

    lax.fori_loop(1, k_ref.shape[0], step, 0)


def attend_back(vis, vat, query, keys, values, grad, out, lse):
    rows, width = query.shape
    heads = width // HD
    smem = pl.BlockSpec(memory_space=pltpu.SMEM)
    vmem = pl.BlockSpec(memory_space=pltpu.VMEM)
    return pl.pallas_call(
        attend_back_kernel,
        out_shape=(
            jax.ShapeDtypeStruct((rows, width), F32),
            jax.ShapeDtypeStruct(keys.shape, BF),
            jax.ShapeDtypeStruct(values.shape, BF),
        ),
        in_specs=[smem, smem] + [vmem] * 6,
        out_specs=(vmem, vmem, vmem),
        scratch_shapes=[pltpu.VMEM((heads, rows, 1), F32)],
        compiler_params=pltpu.CompilerParams(vmem_limit_bytes=48 * 2**20),
        cost_estimate=pl.CostEstimate(
            flops=10 * rows * width * 2048,
            bytes_accessed=16 * 2**20,
            transcendentals=rows * 6 * 2048,
        ),
    )(vis, vat, query, keys, values, grad, out, lse)


def shards(
    tokens,
    cotangent,
    norm_gain,
    w_query,
    b_query,
    w_key,
    b_key,
    w_value,
    b_value,
    w_out,
    ffn_gain,
    w_gate,
    w_up,
    w_down,
    unit_seq,
    block_map,
):
    rows, model = tokens.shape
    blocks = block_map.shape[0]
    bits = blocks.bit_length() - 1
    high = list(range(3, bits))
    low_rows = rows // 2
    width = w_query.shape[1]
    heads = width // HD
    hidden_here = w_gate.shape[1]
    slab = w_gate.shape[0]
    part = -(-hidden_here // 512) * 128
    core = lax.axis_index("mp")
    cube_a = lax.axis_index("a")
    cross = [(1, 2), (2, 1)]
    me = lax.axis_index(("h", "a", "y", "x"))

    order_k = tuple(reversed(high)) + (2, 0, 1)
    order_v = tuple(reversed(high)) + (2, 1, 0)
    place_k = slot_places(order_k)
    place_v = slot_places(order_v)
    vat = jnp.array([place_v.index(s) for s in place_k], jnp.int32)
    per_unit = SEG // rows
    units = jnp.arange(unit_seq.shape[0], dtype=jnp.int32)
    previous = jnp.concatenate([jnp.full((1,), -1, jnp.int32), unit_seq[:-1]])
    first_unit = lax.cummax(jnp.where(unit_seq != previous, units, 0), axis=0)
    others = jnp.bitwise_xor(me, jnp.array(place_k, jnp.int32))
    logical = look(block_map, others)
    seqs = look(unit_seq, logical // per_unit)
    vis = ((seqs == seqs[0]) & (logical < logical[0])).astype(jnp.int32)
    begin = look(first_unit, logical[:1] // per_unit)
    position = logical[0] * rows - begin[0] * SEG + jnp.arange(rows, dtype=jnp.int32)
    cosine, sine = rope_tables(position)

    w_one = w_query[:, : width - 2 * HD]
    w_two = jnp.concatenate([w_query[:, width - 2 * HD :], w_key, w_value], axis=1)
    order_w1 = tuple(reversed(high)) + (2, 0, 1)
    order_w2 = tuple(reversed(high)) + (2, 1, 0)
    w_one = gather_bits(w_one, order_w1)
    w_two = gather_bits(w_two, order_w2)
    out_t = w_out.T
    half_out = width // 2
    out_one = gather_bits(out_t[:, :half_out], order_w1)
    out_two = gather_bits(out_t[:, half_out:], order_w2)
    out_full = jnp.concatenate([out_one, out_two], axis=1)

    def quarter(weight):
        weight = jnp.pad(weight, ((0, 0), (0, 4 * part - hidden_here)))
        return weight.reshape(slab, 4, part).transpose(1, 0, 2)

    def spread(pack):
        other = lax.ppermute(pack, ("a", "mp"), cross)
        pack = jnp.where(cube_a == core, pack, other)
        pack = lax.all_to_all(pack, ("y", "x"), 0, 0, tiled=True)
        pack = pack.reshape(1, -1, pack.shape[-1])
        for bit in high:
            other = flip(pack, bit)
            pack = jnp.where(
                mine(bit) == 0,
                jnp.concatenate([pack, other], 0),
                jnp.concatenate([other, pack], 0),
            )
        other = swap_mp(pack)
        pack = jnp.where(
            core == 0, jnp.stack([pack, other], 1), jnp.stack([other, pack], 1)
        )
        return pack.reshape(-1, pack.shape[-1])

    def collect(grad):
        n = grad.shape[-1]
        grad = grad.reshape(blocks // 8, 2, 4 * slab, n)
        keep = lax.dynamic_index_in_dim(grad, core, 1, keepdims=False)
        send = lax.dynamic_index_in_dim(grad, 1 - core, 1, keepdims=False)
        grad = (keep.astype(F32) + swap_mp(send).astype(F32)).astype(BF)
        for bit in reversed(high):
            grad = grad.reshape(2, -1, 4 * slab, n)
            keep = halves(grad, mine(bit))
            send = halves(grad, 1 - mine(bit))
            grad = (keep.astype(F32) + flip(send, bit).astype(F32)).astype(BF)
        grad = grad.reshape(4, slab, n)
        grad = lax.all_to_all(grad, ("y", "x"), 0, 0, tiled=True)
        other = lax.ppermute(grad, ("a", "mp"), cross)
        return jnp.where(cube_a == core, grad, other)

    def unpack(grad):
        return grad.transpose(1, 0, 2).reshape(slab, 4 * part)[:, :hidden_here].astype(F32)

    gate_up = spread(jnp.concatenate([quarter(w_gate), quarter(w_up)], axis=2))
    down_t = spread(quarter(w_down.T))

    def my_half(value):
        return halves(value.reshape((2, low_rows) + value.shape[1:]), core)

    cot_cube = cube_gather(my_half(cotangent))

    inputs = tokens.astype(F32)
    gain_one = norm_gain.astype(F32)
    inverse_one = lax.rsqrt(jnp.mean(inputs * inputs, axis=-1, keepdims=True) + epsilon)
    normed = (inputs * inverse_one * gain_one).astype(BF)
    lin_two = dot(normed, w_two)
    key_lin = lin_two[:, 2 * HD : 3 * HD] + b_key.astype(F32)
    value_low = (lin_two[:, 3 * HD :] + b_value.astype(F32)).astype(BF)
    key_rot = rotate(key_lin, cosine[:, 0], sine[:, 0]).astype(BF)
    keys = slot_gather(key_rot[None], order_k)
    values = slot_gather(value_low[None], order_v)
    lin_one = dot(normed, w_one)
    query_lin = jnp.concatenate([lin_one, lin_two[:, : 2 * HD]], axis=1) + b_query.astype(F32)
    query = (
        rotate(query_lin.reshape(rows, heads, HD), cosine, sine).reshape(rows, width).astype(BF)
    )
    attended, attended_low, lse = attend(vis, vat, query, keys, values)
    attn = dot(attended_low, out_full, NT).astype(BF).reshape(2, low_rows, model)
    attn = halves(attn, core).astype(F32) + swap_mp(halves(attn, 1 - core)).astype(F32)
    middle = my_half(tokens).astype(F32) + attn
    gain_two = ffn_gain.astype(F32)
    inverse_two = lax.rsqrt(jnp.mean(middle * middle, axis=-1, keepdims=True) + epsilon)
    normed_two = (middle * inverse_two * gain_two).astype(BF)

    cube_two = cube_gather(normed_two)
    grad_hidden = dot(cot_cube, down_t)
    both = dot(cube_two, gate_up)
    gate = both[:, :part]
    up = both[:, part:]
    sigmoid_gate = jax.nn.sigmoid(gate)
    silu_gate = gate * sigmoid_gate
    hidden = (silu_gate * up).astype(BF)
    grad_gate = (grad_hidden * up * sigmoid_gate * (1.0 + gate * (1.0 - sigmoid_gate))).astype(BF)
    grad_up = (grad_hidden * silu_gate).astype(BF)
    grad_both = jnp.concatenate([grad_gate, grad_up], axis=1)
    grad_two = cube_scatter(dot(grad_both, gate_up, NT).astype(BF), low_rows)
    ffn = cube_scatter(dot(hidden, down_t, NT).astype(BF), low_rows)
    mixed_half = (middle + ffn).astype(BF)

    def whole(own):
        other = swap_mp(own)
        return jnp.where(
            core == 0, jnp.concatenate([own, other], 0), jnp.concatenate([other, own], 0)
        )

    mixed = whole(mixed_half)
    grads_down = collect(dot(cot_cube, hidden, TN).astype(BF))
    grads_both = collect(dot(cube_two, grad_both, TN).astype(BF))

    cot_half = my_half(cotangent).astype(F32)
    grad_middle_norm, grad_gain_two = norm_back(grad_two, middle, inverse_two, gain_two)
    grad_middle_half = cot_half + grad_middle_norm
    grad_attn = whole(grad_middle_half.astype(BF))
    grad_middle = whole(grad_middle_half)
    grad_attended = dot(grad_attn, out_full).astype(BF)
    grad_query_rot, grad_keys, grad_values = attend_back(
        vis, vat, query, keys, values, grad_attended, attended, lse
    )
    back_k = tuple(reversed(order_k))
    back_v = tuple(reversed(order_v))
    grad_key_mine = slot_scatter(grad_keys, back_k)[0]
    grad_value_mine = slot_scatter(grad_values, back_v)[0]
    grad_q = (
        rotate(grad_query_rot.reshape(rows, heads, HD), cosine, -sine)
        .reshape(rows, width)
        .astype(BF)
    )
    grad_k = rotate(grad_key_mine, cosine[:, 0], -sine[:, 0]).astype(BF)
    grad_v = grad_value_mine.astype(BF)

    def scatter_two(grad):
        at = grad.shape[1] // 2
        return jnp.concatenate(
            [
                scatter_bits(grad[:, :at], tuple(reversed(order_w1)), blocks),
                scatter_bits(grad[:, at:], tuple(reversed(order_w2)), blocks),
            ],
            axis=1,
        ).astype(F32)

    out_part = scatter_two(dot(grad_attn, attended_low, TN).astype(BF))
    query_part = scatter_two(dot(normed, grad_q, TN).astype(BF))
    grad_kv = jnp.concatenate([grad_k, grad_v], axis=1)
    kv_part = scatter_two(dot(normed, grad_kv, TN).astype(BF))
    at = width - 2 * HD
    grad_normed = dot(grad_q[:, :at], w_one, NT) + dot(
        jnp.concatenate([grad_q[:, at:], grad_kv], axis=1), w_two, NT
    )
    grad_normed = grad_normed.astype(BF)
    grad_normed = grad_normed.astype(F32) + swap_mp(grad_normed).astype(F32)
    grad_input_norm, grad_gain_one = norm_back(grad_normed, inputs, inverse_one, gain_one)
    grad_tokens = grad_middle + grad_input_norm
    bias_query = jnp.sum(grad_q.astype(F32), axis=0)
    bias_kv = jnp.sum(grad_kv.astype(F32), axis=0)

    gain_two_sum = grad_gain_two + swap_mp(grad_gain_two)
    small = jnp.concatenate([grad_gain_one, gain_two_sum, bias_query, bias_kv]).reshape(-1, 128)
    for bit in range(bits):
        small = small + flip(small, bit)
    small = small.reshape(-1)
    gain_one_sum = small[:model]
    gain_two_sum = small[model : 2 * model]
    bias_query_sum = small[2 * model : 2 * model + width]
    bias_key_sum = small[2 * model + width : 2 * model + width + HD]
    bias_value_sum = small[2 * model + width + HD :]
    return (
        mixed,
        grad_tokens,
        gain_one_sum,
        query_part,
        bias_query_sum,
        kv_part[:, :HD],
        bias_key_sum,
        kv_part[:, HD:],
        bias_value_sum,
        out_part.T,
        gain_two_sum,
        unpack(grads_both[:, :, :part]),
        unpack(grads_both[:, :, part:]),
        unpack(grads_down).T,
    )


def solution(mesh):
    blocks, cores = mesh.devices.shape
    mesh = Mesh(
        mesh.devices.reshape(blocks // 8, 2, 2, 2, cores), ("h", "a", "y", "x", "mp")
    )
    blk = ("h", "a", "y", "x")
    placed = (
        P(blk, None),
        P(blk, None),
        P(),
        P(blk, "mp"),
        P("mp"),
        P(blk, "mp"),
        P("mp"),
        P(blk, "mp"),
        P("mp"),
        P("mp", blk),
        P(),
        P(blk, "mp"),
        P(blk, "mp"),
        P("mp", blk),
        P(),
        P(),
    )
    return jax.shard_map(
        shards,
        mesh=mesh,
        in_specs=placed,
        out_specs=(
            P(blk, None),
            P(blk, None),
            P(),
            P(blk, "mp"),
            P("mp"),
            P(blk, "mp"),
            P("mp"),
            P(blk, "mp"),
            P("mp"),
            P("mp", blk),
            P(),
            P(blk, "mp"),
            P(blk, "mp"),
            P("mp", blk),
        ),
        check_vma=False,
    )
```

```python
import functools

import jax
import jax.numpy as jnp
from jax import lax
from jax.experimental import pallas as pl
from jax.experimental.pallas import tpu as pltpu
from jax.sharding import Mesh
from jax.sharding import PartitionSpec as P

HD = 128
SEG = 1024
LOG2E = 1.4426950408889634
BIG = -1e30
BF = jnp.bfloat16
F32 = jnp.float32

epsilon = 1e-06


BLK = ("h", "a", "y", "x")
CUBE_AXES = ("a", "y", "x")


def bit_axis(bit):
    return ("x", "y", "a")[bit] if bit < 3 else "h", 1 if bit < 3 else 1 << (bit - 3)


def flip(value, bit):
    axis, mask = bit_axis(bit)
    return lax.ppermute(value, axis, [(i, i ^ mask) for i in range(lax.axis_size(axis))])


def mine(bit):
    axis, mask = bit_axis(bit)
    return (lax.axis_index(axis) // mask) % 2


def swap_mp(value):
    return lax.ppermute(value, "mp", [(0, 1), (1, 0)])


def halves(value, which):
    return lax.dynamic_index_in_dim(value, which, 0, keepdims=False)


def trade(value, axes, dim=0):
    return lax.all_to_all(value, axes, dim, dim, tiled=True)


def after(value, *others):
    return lax.optimization_barrier((value,) + others)[0]


def together(values):
    return list(lax.optimization_barrier(tuple(values)))


class Gather:
    def __init__(self, value):
        self.value, self.have = value, []

    def step(self, bit):
        at = sum(1 for b in self.have if b > bit)
        other = flip(self.value, bit)
        self.last = other
        self.value = jnp.where(
            mine(bit) == 0,
            jnp.stack([self.value, other], at),
            jnp.stack([other, self.value], at),
        )
        self.have.append(bit)
        return self

    def split(self, count):
        parts = []
        for value in jnp.split(self.value, count, axis=-1):
            part = Gather(value)
            part.have = list(self.have)
            parts.append(part)
        return parts

    def rows(self):
        return self.value.reshape((-1, self.value.shape[-1]))


class Scatter:
    def __init__(self, value, bits):
        self.have = list(range(bits))[::-1]
        self.value = value.reshape((2,) * bits + (-1, value.shape[-1]))

    def step(self, bit, *others):
        at = self.have.index(bit)
        me = mine(bit)
        keep = lax.dynamic_index_in_dim(self.value, me, at, keepdims=False)
        send = lax.dynamic_index_in_dim(self.value, 1 - me, at, keepdims=False)
        self.last = flip(send, bit)
        if others:
            self.last = after(self.last, *others)
        self.value = keep.astype(F32) + self.last.astype(F32)
        self.have.remove(bit)
        if self.have:
            self.value = self.value.astype(BF)
        return self


def joined(parts):
    one = Gather(jnp.concatenate([p.value for p in parts], axis=-1))
    one.have = list(parts[0].have)
    return one


CUBE = ((0, 1, 2), (1, 2, 0), (2, 0, 1))


def cube_parts(rows):
    units = rows // 8
    sizes = [(units + 2 - i) // 3 * 8 for i in range(3)]
    return sizes


def cube_gather(value):
    parts, at = [], 0
    for size in cube_parts(value.shape[0]):
        parts.append(value[at : at + size])
        at += size
    for step in range(3):
        came = together([flip(part, order[step]) for part, order in zip(parts, CUBE)])
        parts = [jnp.concatenate(both, 0) for both in zip(parts, came)]
    return jnp.concatenate(parts, 0), came


class Cube:
    def __init__(self, value):
        self.value, self.size, self.have = value, value.shape[0], [0]

    def step(self, bit):
        self.last = flip(self.value, bit)
        self.value = jnp.concatenate([self.value, self.last], 0)
        self.have = self.have + [h ^ (1 << bit) for h in self.have]
        return self

    def done(self):
        slots = self.value.reshape((8, self.size) + self.value.shape[1:])
        pieces, at = [], 0
        for rows, order in zip(cube_parts(self.size), CUBE):
            wanted = [0]
            for bit in order:
                wanted = wanted + [w ^ (1 << bit) for w in wanted]
            pieces += [slots[self.have.index(w), at : at + rows] for w in wanted]
            at += rows
        return jnp.concatenate(pieces, 0)


class CubeBack:
    def __init__(self, value, rows):
        have = [0]
        for bit in (2, 0, 1):
            have = have + [h ^ (1 << bit) for h in have]
        pieces, at = {}, 0
        for size, order in zip(cube_parts(rows), CUBE):
            wanted = [0]
            for bit in order:
                wanted = wanted + [w ^ (1 << bit) for w in wanted]
            for w in wanted:
                pieces.setdefault(w, []).append(value[at : at + size])
                at += size
        self.value = jnp.concatenate([p for w in have for p in pieces[w]], 0)

    def step(self, bit, *others):
        half = self.value.shape[0] // 2
        other = flip(self.value[half:], bit)
        if others:
            other = after(other, *others)
        self.value = self.value[:half].astype(F32) + other.astype(F32)
        if bit != 2:
            self.value = self.value.astype(BF)
        return self


def cube_scatter(value, rows):
    parts, at, came = [], 0, []
    for size in cube_parts(rows):
        parts.append(value[at : at + 8 * size])
        at += 8 * size
    for step in range(3):
        half = [part.shape[0] // 2 for part in parts]
        sent = [flip(p[n:], order[2 - step]) for p, n, order in zip(parts, half, CUBE)]
        came.append(together(sent))
        parts = [p[:n].astype(F32) + v.astype(F32) for p, n, v in zip(parts, half, came[-1])]
        if step < 2:
            parts = [p.astype(BF) for p in parts]
    return jnp.concatenate(parts, 0), came


def rotate(value, cosine, sine):
    half = value.shape[-1] // 2
    return value * cosine + jnp.concatenate([value[:, half:], value[:, :half]], axis=1) * sine


def rope_tables(position):
    freq = jnp.power(10000.0, -(jnp.arange(HD // 2, dtype=F32) * (2.0 / HD)))
    angle = position.astype(F32)[:, None] * freq[None, :]
    cosine, sine = jnp.cos(angle), jnp.sin(angle)
    return (jnp.concatenate([cosine, cosine], 1), jnp.concatenate([-sine, sine], 1))


def look(table, index):
    places = jnp.arange(table.shape[0], dtype=jnp.int32)
    return jnp.sum(jnp.where(index[:, None] == places[None, :], table[None, :], 0), axis=1)


def norm_back(grad, value, inverse, gain):
    scaled = grad * gain
    grad_gain = jnp.sum(grad * value * inverse, axis=0)
    mean_term = jnp.mean(scaled * value, axis=-1, keepdims=True)
    grad_value = inverse * scaled - value * (inverse * inverse * inverse) * mean_term
    return (grad_value, grad_gain)


NT = (((1,), (1,)), ((), ()))
TN = (((0,), (0,)), ((), ()))


def dot(left, right, dims=(((1,), (0,)), ((), ()))):
    return lax.dot_general(left, right, dims, preferred_element_type=F32)


def own_mask(rows):
    return lax.broadcasted_iota(jnp.int32, (rows, rows), 0) >= lax.broadcasted_iota(
        jnp.int32, (rows, rows), 1
    )


def attend_kernel(vis, q_ref, kv_ref, o_ref, low_ref, lse_ref, acc, top, tot):
    rows, width = q_ref.shape
    heads = width // HD
    blocks = kv_ref.shape[0]
    factor = HD ** (-0.5) * LOG2E

    def block(place, first):
        key = kv_ref[place, :, :HD]
        value = kv_ref[place, :, HD:]
        if first:
            mask = own_mask(rows)
        for h in range(heads):
            cols = slice(h * HD, (h + 1) * HD)
            scores = dot(q_ref[:, cols], key, NT) * factor
            if first:
                scores = jnp.where(mask, scores, BIG)
                best = jnp.max(scores, axis=1, keepdims=True)
                weights = jnp.exp2(scores - best)
                tot[h] = jnp.sum(weights, axis=1, keepdims=True)
                acc[:, cols] = dot(weights.astype(BF), value)
            else:
                old = top[h]
                best = jnp.maximum(old, jnp.max(scores, axis=1, keepdims=True))
                weights = jnp.exp2(scores - best)
                scale = jnp.exp2(old - best)
                tot[h] = tot[h] * scale + jnp.sum(weights, axis=1, keepdims=True)
                acc[:, cols] = acc[:, cols] * scale + dot(weights.astype(BF), value)
            top[h] = best

    block(vis[blocks], True)

    def step(place, carry):
        @pl.when(vis[place] == 1)
        def _():
            block(place, False)

        return carry

    lax.fori_loop(0, blocks, step, 0)
    for h in range(heads):
        cols = slice(h * HD, (h + 1) * HD)
        total = tot[h]
        out = acc[:, cols] / total
        o_ref[:, cols] = out
        low_ref[:, cols] = out.astype(BF)
        lse_ref[:, cols] = jnp.broadcast_to(top[h] + jnp.log(total) * LOG2E, (rows, HD))


def attend(vis, query, keyval):
    rows, width = query.shape
    heads = width // HD
    smem = pl.BlockSpec(memory_space=pltpu.SMEM)
    vmem = pl.BlockSpec(memory_space=pltpu.VMEM)
    return pl.pallas_call(
        attend_kernel,
        out_shape=(
            jax.ShapeDtypeStruct((rows, width), F32),
            jax.ShapeDtypeStruct((rows, width), BF),
            jax.ShapeDtypeStruct((rows, width), F32),
        ),
        in_specs=[smem, vmem, vmem],
        out_specs=(vmem, vmem, vmem),
        scratch_shapes=[
            pltpu.VMEM((rows, width), F32),
            pltpu.VMEM((heads, rows, 1), F32),
            pltpu.VMEM((heads, rows, 1), F32),
        ],
        compiler_params=pltpu.CompilerParams(vmem_limit_bytes=40 * 2**20),
        cost_estimate=pl.CostEstimate(
            flops=4 * rows * width * 2048, bytes_accessed=8 * 2**20, transcendentals=rows * 6 * 2048
        ),
    )(vis, query, keyval)


def attend_back_kernel(
    vis, q_ref, kv_ref, do_ref, o_ref, lse_ref, cos_ref, sin_ref, out_ref, dkv_ref, dq_ref, delta
):
    rows, width = q_ref.shape
    heads = width // HD
    blocks = kv_ref.shape[0]
    scale = HD ** (-0.5)
    for h in range(heads):
        cols = slice(h * HD, (h + 1) * HD)
        delta[h] = jnp.sum(do_ref[:, cols].astype(F32) * o_ref[:, cols], axis=1, keepdims=True)

    def block(place, first):
        key = kv_ref[place, :, :HD]
        value = kv_ref[place, :, HD:]
        if first:
            mask = own_mask(rows)
        dk = jnp.zeros((rows, HD), F32)
        dv = jnp.zeros((rows, HD), F32)
        for h in range(heads):
            cols = slice(h * HD, (h + 1) * HD)
            query = q_ref[:, cols]
            grad = do_ref[:, cols]
            probs = jnp.exp2(
                dot(query, key, NT) * (scale * LOG2E) - lse_ref[:, h * HD : h * HD + 1]
            )
            if first:
                probs = jnp.where(mask, probs, 0.0)
            dv = dv + dot(probs.astype(BF), grad, TN)
            dprobs = dot(grad, value, NT)
            dscores = (probs * (dprobs - delta[h])).astype(BF)
            dk = dk + dot(dscores, query, TN)
            dq = dot(dscores, key) * scale
            if first:
                dq_ref[:, cols] = dq
            else:
                dq_ref[:, cols] = dq_ref[:, cols] + dq
        dkv_ref[place, :, :HD] = (dk * scale).astype(BF)
        dkv_ref[place, :, HD:] = dv.astype(BF)

    block(vis[blocks], True)

    def step(place, carry):
        @pl.when(vis[place] == 1)
        def _():
            block(place, False)

        @pl.when((vis[place] == 0) & (place != vis[blocks]))
        def _():
            dkv_ref[place] = jnp.zeros((rows, 2 * HD), BF)

        return carry

    lax.fori_loop(0, blocks, step, 0)
    for h in range(heads):
        cols = slice(h * HD, (h + 1) * HD)
        out_ref[:, cols] = turn(dq_ref[:, cols], cos_ref[...], -sin_ref[...]).astype(BF)


def attend_back(vis, query, keyval, grad, out, lse, cosine, sine):
    rows, width = query.shape
    heads = width // HD
    smem = pl.BlockSpec(memory_space=pltpu.SMEM)
    vmem = pl.BlockSpec(memory_space=pltpu.VMEM)
    return pl.pallas_call(
        attend_back_kernel,
        out_shape=(
            jax.ShapeDtypeStruct((rows, width), BF),
            jax.ShapeDtypeStruct(keyval.shape, BF),
        ),
        in_specs=[smem] + [vmem] * 7,
        out_specs=(vmem, vmem),
        scratch_shapes=[
            pltpu.VMEM((rows, width), F32),
            pltpu.VMEM((heads, rows, 1), F32),
        ],
        compiler_params=pltpu.CompilerParams(vmem_limit_bytes=48 * 2**20),
        cost_estimate=pl.CostEstimate(
            flops=10 * rows * width * 2048,
            bytes_accessed=16 * 2**20,
            transcendentals=rows * 6 * 2048,
        ),
    )(vis, query, keyval, grad, out, lse, cosine, sine)


def turn(value, cosine, sine):
    return value * cosine + pltpu.roll(value, HD // 2, 1) * sine


def project_kernel(turned, x_ref, w_ref, b_ref, cos_ref, sin_ref, o_ref):
    lin = dot(x_ref[...], w_ref[...]) + b_ref[...]
    for h in range(lin.shape[1] // HD):
        cols = slice(h * HD, (h + 1) * HD)
        head = lin[:, cols]
        if h < turned:
            head = turn(head, cos_ref[...], sin_ref[...])
        o_ref[:, cols] = head.astype(BF)


def project(normed, weight, bias, cosine, sine, turned):
    rows = normed.shape[0]
    width = weight.shape[1]
    vmem = pl.BlockSpec(memory_space=pltpu.VMEM)
    return pl.pallas_call(
        functools.partial(project_kernel, turned),
        out_shape=jax.ShapeDtypeStruct((rows, width), BF),
        in_specs=[vmem] * 5,
        out_specs=vmem,
        compiler_params=pltpu.CompilerParams(vmem_limit_bytes=24 * 2**20),
        cost_estimate=pl.CostEstimate(
            flops=2 * rows * width * normed.shape[1],
            bytes_accessed=2 * normed.shape[1] * (rows + width),
            transcendentals=0,
        ),
    )(normed, weight, bias.astype(F32)[None], cosine, sine)


def share(tiles, chip):
    at = (chip * tiles) // 8
    return at, ((chip + 1) * tiles) // 8 - at


def pack_kernel(tiles, part, gate_ref, up_ref, down_ref, both_out, down_out):
    at, count = share(tiles, pl.program_id(0))
    cols = pl.ds(pl.multiple_of(at * 128, 128), part)
    keep = lax.broadcasted_iota(jnp.int32, (gate_ref.shape[0], part), 1) < count * 128

    def kept(value):
        return jnp.where(keep, value.astype(F32), 0.0).astype(BF)

    both_out[0, :, :part] = kept(gate_ref[:, cols])
    both_out[0, :, part:] = kept(up_ref[:, cols])
    down_out[0] = kept(down_ref[cols, :].astype(F32).T)


def pack(w_gate, w_up, w_down, part):
    slab, hidden = w_gate.shape
    vmem = pl.BlockSpec(memory_space=pltpu.VMEM)
    return pl.pallas_call(
        functools.partial(pack_kernel, hidden // 128, part),
        grid=(8,),
        out_shape=(
            jax.ShapeDtypeStruct((8, slab, 2 * part), BF),
            jax.ShapeDtypeStruct((8, slab, part), BF),
        ),
        in_specs=[vmem] * 3,
        out_specs=(
            pl.BlockSpec((1, slab, 2 * part), lambda c: (c, 0, 0)),
            pl.BlockSpec((1, slab, part), lambda c: (c, 0, 0)),
        ),
        compiler_params=pltpu.CompilerParams(vmem_limit_bytes=24 * 2**20),
        cost_estimate=pl.CostEstimate(flops=0, bytes_accessed=8 * 2**20, transcendentals=0),
    )(w_gate, w_up, w_down)


def unpack_kernel(tiles, gate_ref, up_ref, down_ref, gate_out, up_out, down_out):
    for c in range(8):
        at, size = share(tiles, c)
        here, width = slice(at * 128, (at + size) * 128), size * 128
        gate_out[:, here] = gate_ref[c, :, :width].astype(F32)
        up_out[:, here] = up_ref[c, :, :width].astype(F32)
        down_out[here, :] = down_ref[c, :, :width].astype(F32).T


def unpack(gate, up, down, hidden):
    slab = down.shape[1]
    vmem = pl.BlockSpec(memory_space=pltpu.VMEM)
    return pl.pallas_call(
        functools.partial(unpack_kernel, hidden // 128),
        out_shape=(
            jax.ShapeDtypeStruct((slab, hidden), F32),
            jax.ShapeDtypeStruct((slab, hidden), F32),
            jax.ShapeDtypeStruct((hidden, slab), F32),
        ),
        in_specs=[vmem] * 3,
        out_specs=(vmem,) * 3,
        compiler_params=pltpu.CompilerParams(vmem_limit_bytes=40 * 2**20),
        cost_estimate=pl.CostEstimate(flops=0, bytes_accessed=10 * 2**20, transcendentals=0),
    )(gate, up, down)


def shards(
    tokens,
    cotangent,
    norm_gain,
    w_query,
    b_query,
    w_key,
    b_key,
    w_value,
    b_value,
    w_out,
    ffn_gain,
    w_gate,
    w_up,
    w_down,
    unit_seq,
    block_map,
):
    rows, model = tokens.shape
    blocks = block_map.shape[0]
    low_rows = rows // 2
    width = w_query.shape[1]
    heads = width // HD
    slab = w_gate.shape[0]
    tiles = w_gate.shape[1] // 128
    part = -(-tiles // 8) * 128
    core = lax.axis_index("mp")
    me = lax.axis_index(BLK)

    def my_half(value):
        return halves(value.reshape((2, low_rows) + value.shape[1:]), core)

    bits = blocks.bit_length() - 1
    high = list(range(3, bits))[::-1]

    both_send, down_send = pack(w_gate, w_up, w_down, part)
    w_kv = Gather(jnp.concatenate([w_key, w_value], axis=1))
    w_q = Gather(w_query)
    w_out_all = Gather(w_out.T)
    cot_half = my_half(cotangent)
    cot_cube = Cube(cot_half)
    for bit in high:
        w_kv.step(bit)
        w_q.step(bit)
        w_out_all.step(bit)
    cot_cube.step(1)
    both_cube = trade(after(both_send, w_kv.last, w_q.last), CUBE_AXES)
    down_cube = trade(after(down_send, both_cube), CUBE_AXES)
    both_own = lax.all_gather(both_cube.reshape(8 * slab, -1), "h", axis=0, tiled=True)
    down_own = lax.all_gather(down_cube.reshape(8 * slab, -1), "h", axis=0, tiled=True)
    block_map = after(block_map, both_send)
    inputs = after(tokens, both_send).astype(F32)
    per_unit = SEG // rows
    units = jnp.arange(unit_seq.shape[0], dtype=jnp.int32)
    previous = jnp.concatenate([jnp.full((1,), -1, jnp.int32), unit_seq[:-1]])
    first_unit = lax.cummax(jnp.where(unit_seq != previous, units, 0), axis=0)
    seqs = look(unit_seq, block_map // per_unit)
    own_place = jnp.arange(blocks, dtype=jnp.int32) == me
    my_block = jnp.sum(jnp.where(own_place, block_map, 0))
    my_seq = jnp.sum(jnp.where(own_place, seqs, 0))
    vis = ((seqs == my_seq) & (block_map < my_block)).astype(jnp.int32)
    vis = jnp.concatenate([vis, me[None].astype(jnp.int32)])
    begin = look(first_unit, (my_block // per_unit)[None])
    position = my_block * rows - begin[0] * SEG + jnp.arange(rows, dtype=jnp.int32)
    cosine, sine = rope_tables(position)

    gain_one = norm_gain.astype(F32)
    inverse_one = lax.rsqrt(jnp.mean(inputs * inputs, axis=-1, keepdims=True) + epsilon)
    normed = (inputs * inverse_one * gain_one).astype(BF)
    w_kv.value = after(w_kv.value, both_cube, cosine, vis, normed, cot_cube.last, w_out_all.last)
    w_q.value = after(w_q.value, both_cube)
    w_kv.step(2)
    w_q.step(2)
    one, two = w_q.split(2)
    w_kv.step(1)
    one.step(0)
    two.step(1)
    cot_cube.value = after(cot_cube.value, w_q.last)
    cot_cube.step(2)
    w_kv = w_kv.step(0).rows()
    w_q = joined([one.step(1), two.step(0)]).rows()

    keyval = Gather(project(normed, w_kv, jnp.concatenate([b_key, b_value]), cosine, sine, 1))

    w_out_all.value = after(w_out_all.value, w_kv)
    for bit in high:
        keyval.step(bit)
    w_out_all.step(2)
    keyval.value = after(keyval.value, down_cube, w_out_all.last, cot_cube.last)
    keyval.step(2)
    w_out_all.step(0)
    key_part, value_part = keyval.split(2)
    key_part.value = after(key_part.value, w_out_all.last)
    key_part.step(0)
    value_part.step(1)
    key_part.step(1)
    value_part.step(0)
    w_out_all.value = after(w_out_all.value, key_part.last, value_part.last)
    cot_cube.value = after(cot_cube.value, key_part.last, value_part.last)
    keyval = joined([key_part, value_part]).value.reshape(blocks, rows, 2 * HD)
    out_full = w_out_all.step(1).rows()
    cot_cube.step(0)
    query = project(normed, w_q, b_query, cosine, sine, heads)
    attended, attended_low, lse = attend(vis, query, keyval)
    attended_low = after(attended_low, cot_cube.last)
    cot_cube = cot_cube.done()
    attn = dot(attended_low, out_full, NT).astype(BF).reshape(2, low_rows, model)
    attn = halves(attn, core).astype(F32) + swap_mp(halves(attn, 1 - core)).astype(F32)
    middle = my_half(tokens).astype(F32) + attn
    gain_two = ffn_gain.astype(F32)
    inverse_two = lax.rsqrt(jnp.mean(middle * middle, axis=-1, keepdims=True) + epsilon)
    normed_two = (middle * inverse_two * gain_two).astype(BF)
    cube_two, came = cube_gather(normed_two)
    both_w = (both_own, swap_mp(both_own))
    down_w = (down_own, swap_mp(down_own))

    def collect(mine, theirs):
        return (mine + swap_mp(theirs.astype(BF)).astype(F32)).astype(BF)

    def over_high_back(value):
        return lax.psum_scatter(value, "h", scatter_dimension=0, tiled=True)

    lins, hiddens, grads = [], [], []
    for both in both_w:
        lin = dot(cube_two, both)
        gate, up = lin[:, :part], lin[:, part:]
        sigmoid_gate = jax.nn.sigmoid(gate)
        silu_gate = gate * sigmoid_gate
        hiddens.append((silu_gate * up).astype(BF))
        lins.append((gate, up, sigmoid_gate, silu_gate))
    down_back = collect(dot(cot_cube, hiddens[0], TN), dot(cot_cube, hiddens[1], TN))
    down_high = over_high_back(down_back)
    for (gate, up, sigmoid_gate, silu_gate), down in zip(lins, down_w):
        grad_hidden = dot(cot_cube, down)
        grad_gate = grad_hidden * up * sigmoid_gate * (1.0 + gate * (1.0 - sigmoid_gate))
        grad_up = grad_hidden * silu_gate
        grads.append(jnp.concatenate([grad_gate.astype(BF), grad_up.astype(BF)], axis=1))
    grad_two = dot(grads[0], both_w[0], NT) + dot(grads[1], both_w[1], NT)
    grad_two = grad_two.astype(BF)
    grads = [after(v, grad_two) for v in grads]
    both_mine, both_theirs = dot(cube_two, grads[0], TN), dot(cube_two, grads[1], TN)
    both_theirs = swap_mp(both_theirs.astype(BF)).astype(F32)
    gate_back = (both_mine[:, :part] + both_theirs[:, :part]).astype(BF)
    up_back = (both_mine[:, part:] + both_theirs[:, part:]).astype(BF)
    gate_high = over_high_back(gate_back)
    up_high = over_high_back(up_back)
    kept = [after(v, grad_two) for v in hiddens]
    grad_two, came = cube_scatter(grad_two, low_rows)
    grad_two = after(grad_two, down_back, gate_back, up_back)
    ffn = dot(kept[0], down_w[0], NT) + dot(kept[1], down_w[1], NT)
    ffn = CubeBack(after(ffn.astype(BF), *came[2]), low_rows)

    def whole(own):
        other = swap_mp(own)
        return jnp.where(
            core == 0, jnp.concatenate([own, other], 0), jnp.concatenate([other, own], 0)
        )

    grad_middle_norm, grad_gain_two = norm_back(grad_two, middle, inverse_two, gain_two)
    grad_middle_half = cot_half.astype(F32) + grad_middle_norm
    grad_attn = whole(grad_middle_half.astype(BF))
    grad_middle = whole(grad_middle_half)
    grad_attended = dot(grad_attn, out_full).astype(BF)
    out_grad = dot(grad_attn, attended_low, TN).astype(BF)
    grad_q, grad_kv_all = attend_back(
        vis, query, keyval, grad_attended, attended, lse, cosine, sine
    )
    low = [2] + high[::-1]

    def pair(grad):
        n = grad.shape[1] // 2
        return [Scatter(grad[:, :n], bits), Scatter(grad[:, n:], bits)]

    def merge(parts):
        parts[0].value = jnp.concatenate([p.value for p in parts], axis=-1)
        return parts[0]

    def hold(parts, *others):
        for p in parts:
            p.value = after(p.value, *others)

    ffn.step(1, grad_q)
    out_sum = pair(out_grad)
    out_sum[0].step(0, grad_q)
    out_sum[1].step(1, grad_q)
    kv_sum = pair(grad_kv_all.reshape(blocks * rows, 2 * HD))
    kv_sum[0].step(0)
    kv_sum[1].step(1)
    hold(out_sum, kv_sum[0].last, kv_sum[1].last)
    kv_sum[0].step(1)
    kv_sum[1].step(0)
    kv_sum = merge(kv_sum)
    out_sum[0].step(1)
    out_sum[1].step(0)
    out_sum = merge(out_sum)
    query_sum = pair(dot(normed, grad_q, TN).astype(BF))
    hold(query_sum, kv_sum.last)
    hold([ffn], kv_sum.last)
    query_sum[0].step(0)
    query_sum[1].step(1)
    ffn.step(0)
    kv_sum.step(2)
    out_sum.step(2)
    hold([kv_sum], query_sum[0].last, query_sum[1].last, out_sum.last)
    for bit in high[::-1]:
        kv_sum.step(bit)
        out_sum.step(bit)
    kv_mine = kv_sum.value
    hold(query_sum, kv_sum.last)
    hold([ffn], kv_sum.last)
    query_sum[0].step(1)
    query_sum[1].step(0)
    query_sum = merge(query_sum)
    ffn.step(2)
    mixed = whole((middle + ffn.value).astype(BF))
    grad_k = rotate(kv_mine[:, :HD], cosine, -sine).astype(BF)
    grad_v = kv_mine[:, HD:].astype(BF)
    grad_kv = jnp.concatenate([grad_k, grad_v], axis=1)
    last = Scatter(dot(normed, grad_kv, TN).astype(BF), bits)
    grad_normed = (dot(grad_q, w_q, NT) + dot(grad_kv, w_kv, NT)).astype(BF)
    other_normed = swap_mp(grad_normed)
    last.step(1)
    grad_normed = grad_normed.astype(F32) + other_normed.astype(F32)
    grad_input_norm, grad_gain_one = norm_back(grad_normed, inputs, inverse_one, gain_one)
    bias_query = jnp.sum(grad_q.astype(F32), axis=0)
    bias_kv = jnp.sum(grad_kv.astype(F32), axis=0)
    gain_two_sum = grad_gain_two + swap_mp(grad_gain_two)
    small = jnp.concatenate([grad_gain_one, gain_two_sum, bias_query, bias_kv]).reshape(-1, 128)
    hold([last], query_sum.last, other_normed)
    last.step(0)
    query_sum.step(2)
    came = flip(small, 0)
    small = small + came
    hold([last], came)
    last.step(2)
    came = flip(small, 1)
    small = small + came
    hold([last], came)
    for bit in high[::-1]:
        query_sum.step(bit)
        last.step(bit)
    for bit in range(2, bits):
        small = small + flip(small, bit)
    small = small.reshape(-1)
    out_part, query_part, kv_part = out_sum.value, query_sum.value, last.value

    def home(value, *others):
        return trade(after(value, *others).reshape(8, slab, part), CUBE_AXES)

    down_back = home(down_high)
    gate_back = home(gate_high, down_back)
    up_back = home(up_high, gate_back)
    gate_part, up_part, down_part = unpack(gate_back, up_back, down_back, w_gate.shape[1])
    grad_tokens = grad_middle + grad_input_norm
    gain_one_sum = small[:model]
    gain_two_sum = small[model : 2 * model]
    bias_query_sum = small[2 * model : 2 * model + width]
    bias_key_sum = small[2 * model + width : 2 * model + width + HD]
    bias_value_sum = small[2 * model + width + HD :]
    return (
        mixed,
        grad_tokens,
        gain_one_sum,
        query_part,
        bias_query_sum,
        kv_part[:, :HD],
        bias_key_sum,
        kv_part[:, HD:],
        bias_value_sum,
        out_part.T,
        gain_two_sum,
        gate_part,
        up_part,
        down_part,
    )


def solution(mesh):
    blocks, cores = mesh.devices.shape
    mesh = Mesh(
        mesh.devices.reshape(blocks // 8, 2, 2, 2, cores), ("h", "a", "y", "x", "mp")
    )
    blk = ("h", "a", "y", "x")
    placed = (
        P(blk, None),
        P(blk, None),
        P(),
        P(blk, "mp"),
        P("mp"),
        P(blk, "mp"),
        P("mp"),
        P(blk, "mp"),
        P("mp"),
        P("mp", blk),
        P(),
        P(blk, "mp"),
        P(blk, "mp"),
        P("mp", blk),
        P(),
        P(),
    )
    return jax.shard_map(
        shards,
        mesh=mesh,
        in_specs=placed,
        out_specs=(
            P(blk, None),
            P(blk, None),
            P(),
            P(blk, "mp"),
            P("mp"),
            P(blk, "mp"),
            P("mp"),
            P(blk, "mp"),
            P("mp"),
            P("mp", blk),
            P(),
            P(blk, "mp"),
            P(blk, "mp"),
            P("mp", blk),
        ),
        check_vma=False,
    )
```

```python
import functools

import jax
import jax.numpy as jnp
from jax import lax
from jax.experimental import pallas as pl
from jax.experimental.pallas import tpu as pltpu
from jax.sharding import Mesh
from jax.sharding import PartitionSpec as P

HD = 128
SEG = 1024
LOG2E = 1.4426950408889634
BIG = -1e30
BF = jnp.bfloat16
F32 = jnp.float32

epsilon = 1e-06


BLK = ("h", "a", "y", "x")
CUBE_AXES = ("a", "y", "x")


def bit_axis(bit):
    return ("x", "y", "a")[bit] if bit < 3 else "h", 1 if bit < 3 else 1 << (bit - 3)


def flip(value, bit):
    axis, mask = bit_axis(bit)
    return lax.ppermute(value, axis, [(i, i ^ mask) for i in range(lax.axis_size(axis))])


def mine(bit):
    axis, mask = bit_axis(bit)
    return (lax.axis_index(axis) // mask) % 2


def swap_mp(value):
    return lax.ppermute(value, "mp", [(0, 1), (1, 0)])


def halves(value, which):
    return lax.dynamic_index_in_dim(value, which, 0, keepdims=False)


def trade(value, axes, dim=0):
    return lax.all_to_all(value, axes, dim, dim, tiled=True)


def after(value, *others):
    if not others:
        return value
    return lax.optimization_barrier((value,) + others)[0]


def together(values):
    return list(lax.optimization_barrier(tuple(values)))


class Gather:
    def __init__(self, value):
        self.value, self.have = value, []

    def step(self, bit):
        at = sum(1 for b in self.have if b > bit)
        other = flip(self.value, bit)
        self.last = other
        self.value = jnp.where(
            mine(bit) == 0,
            jnp.stack([self.value, other], at),
            jnp.stack([other, self.value], at),
        )
        self.have.append(bit)
        return self

    def split(self, count):
        parts = []
        for value in jnp.split(self.value, count, axis=-1):
            part = Gather(value)
            part.have = list(self.have)
            parts.append(part)
        return parts

    def rows(self):
        return self.value.reshape((-1, self.value.shape[-1]))


class Scatter:
    def __init__(self, value, bits):
        self.have = list(range(bits))[::-1]
        self.value = value.reshape((2,) * bits + (-1, value.shape[-1]))

    def step(self, bit, *others):
        at = self.have.index(bit)
        me = mine(bit)
        keep = lax.dynamic_index_in_dim(self.value, me, at, keepdims=False)
        send = lax.dynamic_index_in_dim(self.value, 1 - me, at, keepdims=False)
        self.last = flip(send, bit)
        if others:
            self.last = after(self.last, *others)
        self.value = keep.astype(F32) + self.last.astype(F32)
        self.have.remove(bit)
        if self.have:
            self.value = self.value.astype(BF)
        return self


def joined(parts):
    one = Gather(jnp.concatenate([p.value for p in parts], axis=-1))
    one.have = list(parts[0].have)
    return one


CUBE = ((0, 1, 2), (1, 2, 0), (2, 0, 1))


def cube_parts(rows):
    units = rows // 8
    sizes = [(units + 2 - i) // 3 * 8 for i in range(3)]
    return sizes


def cube_gather(value):
    parts, at = [], 0
    for size in cube_parts(value.shape[0]):
        parts.append(value[at : at + size])
        at += size
    for step in range(3):
        came = together([flip(part, order[step]) for part, order in zip(parts, CUBE)])
        parts = [jnp.concatenate(both, 0) for both in zip(parts, came)]
    return jnp.concatenate(parts, 0), came


class Cube:
    def __init__(self, value):
        self.value, self.size, self.have = value, value.shape[0], [0]

    def step(self, bit):
        self.last = flip(self.value, bit)
        self.value = jnp.concatenate([self.value, self.last], 0)
        self.have = self.have + [h ^ (1 << bit) for h in self.have]
        return self

    def done(self):
        slots = self.value.reshape((8, self.size) + self.value.shape[1:])
        pieces, at = [], 0
        for rows, order in zip(cube_parts(self.size), CUBE):
            wanted = [0]
            for bit in order:
                wanted = wanted + [w ^ (1 << bit) for w in wanted]
            pieces += [slots[self.have.index(w), at : at + rows] for w in wanted]
            at += rows
        return jnp.concatenate(pieces, 0)


class CubeSum:
    def __init__(self, value, rows):
        self.parts, self.number, at = [], 0, 0
        for size in cube_parts(rows):
            self.parts.append(value[at : at + 8 * size])
            at += 8 * size

    def step(self, *others):
        half = [part.shape[0] // 2 for part in self.parts]
        sent = [
            flip(after(p[n:], *others), order[2 - self.number])
            for p, n, order in zip(self.parts, half, CUBE)
        ]
        self.came = together(sent)
        self.parts = [
            p[:n].astype(F32) + v.astype(F32) for p, n, v in zip(self.parts, half, self.came)
        ]
        self.number += 1
        if self.number < 3:
            self.parts = [p.astype(BF) for p in self.parts]
        return self

    def total(self):
        return jnp.concatenate(self.parts, 0)


def rotate(value, cosine, sine):
    half = value.shape[-1] // 2
    return value * cosine + jnp.concatenate([value[:, half:], value[:, :half]], axis=1) * sine


def rope_tables(position):
    freq = jnp.power(10000.0, -(jnp.arange(HD // 2, dtype=F32) * (2.0 / HD)))
    angle = position.astype(F32)[:, None] * freq[None, :]
    cosine, sine = jnp.cos(angle), jnp.sin(angle)
    return (jnp.concatenate([cosine, cosine], 1), jnp.concatenate([-sine, sine], 1))


def look(table, index):
    places = jnp.arange(table.shape[0], dtype=jnp.int32)
    return jnp.sum(jnp.where(index[:, None] == places[None, :], table[None, :], 0), axis=1)


def norm_back(grad, value, inverse, gain):
    scaled = grad * gain
    grad_gain = jnp.sum(grad * value * inverse, axis=0)
    mean_term = jnp.mean(scaled * value, axis=-1, keepdims=True)
    grad_value = inverse * scaled - value * (inverse * inverse * inverse) * mean_term
    return (grad_value, grad_gain)


NT = (((1,), (1,)), ((), ()))
TN = (((0,), (0,)), ((), ()))


def dot(left, right, dims=(((1,), (0,)), ((), ()))):
    return lax.dot_general(left, right, dims, preferred_element_type=F32)


def own_mask(rows):
    return lax.broadcasted_iota(jnp.int32, (rows, rows), 0) >= lax.broadcasted_iota(
        jnp.int32, (rows, rows), 1
    )


def attend_kernel(vis, q_ref, kv_ref, o_ref, low_ref, lse_ref, acc, top, tot):
    rows, width = q_ref.shape
    heads = width // HD
    blocks = kv_ref.shape[0]
    factor = HD ** (-0.5) * LOG2E

    def block(place, first):
        key = kv_ref[place, :, :HD]
        value = kv_ref[place, :, HD:]
        if first:
            mask = own_mask(rows)
        for h in range(heads):
            cols = slice(h * HD, (h + 1) * HD)
            scores = dot(q_ref[:, cols], key, NT) * factor
            if first:
                scores = jnp.where(mask, scores, BIG)
                best = jnp.max(scores, axis=1, keepdims=True)
                weights = jnp.exp2(scores - best)
                tot[h] = jnp.sum(weights, axis=1, keepdims=True)
                acc[:, cols] = dot(weights.astype(BF), value)
            else:
                old = top[h]
                best = jnp.maximum(old, jnp.max(scores, axis=1, keepdims=True))
                weights = jnp.exp2(scores - best)
                scale = jnp.exp2(old - best)
                tot[h] = tot[h] * scale + jnp.sum(weights, axis=1, keepdims=True)
                acc[:, cols] = acc[:, cols] * scale + dot(weights.astype(BF), value)
            top[h] = best

    block(vis[blocks], True)

    def step(place, carry):
        @pl.when(vis[place] == 1)
        def _():
            block(place, False)

        return carry

    lax.fori_loop(0, blocks, step, 0)
    for h in range(heads):
        cols = slice(h * HD, (h + 1) * HD)
        total = tot[h]
        out = acc[:, cols] / total
        o_ref[:, cols] = out
        low_ref[:, cols] = out.astype(BF)
        lse_ref[:, cols] = jnp.broadcast_to(top[h] + jnp.log(total) * LOG2E, (rows, HD))


def attend(vis, query, keyval):
    rows, width = query.shape
    heads = width // HD
    smem = pl.BlockSpec(memory_space=pltpu.SMEM)
    vmem = pl.BlockSpec(memory_space=pltpu.VMEM)
    return pl.pallas_call(
        attend_kernel,
        out_shape=(
            jax.ShapeDtypeStruct((rows, width), F32),
            jax.ShapeDtypeStruct((rows, width), BF),
            jax.ShapeDtypeStruct((rows, width), F32),
        ),
        in_specs=[smem, vmem, vmem],
        out_specs=(vmem, vmem, vmem),
        scratch_shapes=[
            pltpu.VMEM((rows, width), F32),
            pltpu.VMEM((heads, rows, 1), F32),
            pltpu.VMEM((heads, rows, 1), F32),
        ],
        compiler_params=pltpu.CompilerParams(vmem_limit_bytes=40 * 2**20),
        cost_estimate=pl.CostEstimate(
            flops=4 * rows * width * 2048, bytes_accessed=8 * 2**20, transcendentals=rows * 6 * 2048
        ),
    )(vis, query, keyval)


def attend_back_kernel(
    vis, q_ref, kv_ref, do_ref, o_ref, lse_ref, cos_ref, sin_ref, out_ref, dkv_ref, dq_ref, delta
):
    rows, width = q_ref.shape
    heads = width // HD
    blocks = kv_ref.shape[0]
    scale = HD ** (-0.5)
    for h in range(heads):
        cols = slice(h * HD, (h + 1) * HD)
        delta[h] = jnp.sum(do_ref[:, cols].astype(F32) * o_ref[:, cols], axis=1, keepdims=True)

    def block(place, first):
        key = kv_ref[place, :, :HD]
        value = kv_ref[place, :, HD:]
        if first:
            mask = own_mask(rows)
        dk = jnp.zeros((rows, HD), F32)
        dv = jnp.zeros((rows, HD), F32)
        for h in range(heads):
            cols = slice(h * HD, (h + 1) * HD)
            query = q_ref[:, cols]
            grad = do_ref[:, cols]
            probs = jnp.exp2(
                dot(query, key, NT) * (scale * LOG2E) - lse_ref[:, h * HD : h * HD + 1]
            )
            if first:
                probs = jnp.where(mask, probs, 0.0)
            dv = dv + dot(probs.astype(BF), grad, TN)
            dprobs = dot(grad, value, NT)
            dscores = (probs * (dprobs - delta[h])).astype(BF)
            dk = dk + dot(dscores, query, TN)
            dq = dot(dscores, key) * scale
            if first:
                dq_ref[:, cols] = dq
            else:
                dq_ref[:, cols] = dq_ref[:, cols] + dq
        dkv_ref[place, :, :HD] = (dk * scale).astype(BF)
        dkv_ref[place, :, HD:] = dv.astype(BF)

    block(vis[blocks], True)

    def step(place, carry):
        @pl.when(vis[place] == 1)
        def _():
            block(place, False)

        @pl.when((vis[place] == 0) & (place != vis[blocks]))
        def _():
            dkv_ref[place] = jnp.zeros((rows, 2 * HD), BF)

        return carry

    lax.fori_loop(0, blocks, step, 0)
    for h in range(heads):
        cols = slice(h * HD, (h + 1) * HD)
        out_ref[:, cols] = turn(dq_ref[:, cols], cos_ref[...], -sin_ref[...]).astype(BF)


def attend_back(vis, query, keyval, grad, out, lse, cosine, sine):
    rows, width = query.shape
    heads = width // HD
    smem = pl.BlockSpec(memory_space=pltpu.SMEM)
    vmem = pl.BlockSpec(memory_space=pltpu.VMEM)
    return pl.pallas_call(
        attend_back_kernel,
        out_shape=(
            jax.ShapeDtypeStruct((rows, width), BF),
            jax.ShapeDtypeStruct(keyval.shape, BF),
        ),
        in_specs=[smem] + [vmem] * 7,
        out_specs=(vmem, vmem),
        scratch_shapes=[
            pltpu.VMEM((rows, width), F32),
            pltpu.VMEM((heads, rows, 1), F32),
        ],
        compiler_params=pltpu.CompilerParams(vmem_limit_bytes=48 * 2**20),
        cost_estimate=pl.CostEstimate(
            flops=10 * rows * width * 2048,
            bytes_accessed=16 * 2**20,
            transcendentals=rows * 6 * 2048,
        ),
    )(vis, query, keyval, grad, out, lse, cosine, sine)


def turn(value, cosine, sine):
    return value * cosine + pltpu.roll(value, HD // 2, 1) * sine


def project_kernel(turned, x_ref, w_ref, b_ref, cos_ref, sin_ref, o_ref):
    lin = dot(x_ref[...], w_ref[...]) + b_ref[...]
    for h in range(lin.shape[1] // HD):
        cols = slice(h * HD, (h + 1) * HD)
        head = lin[:, cols]
        if h < turned:
            head = turn(head, cos_ref[...], sin_ref[...])
        o_ref[:, cols] = head.astype(BF)


def project(normed, weight, bias, cosine, sine, turned):
    rows = normed.shape[0]
    width = weight.shape[1]
    vmem = pl.BlockSpec(memory_space=pltpu.VMEM)
    return pl.pallas_call(
        functools.partial(project_kernel, turned),
        out_shape=jax.ShapeDtypeStruct((rows, width), BF),
        in_specs=[vmem] * 5,
        out_specs=vmem,
        compiler_params=pltpu.CompilerParams(vmem_limit_bytes=24 * 2**20),
        cost_estimate=pl.CostEstimate(
            flops=2 * rows * width * normed.shape[1],
            bytes_accessed=2 * normed.shape[1] * (rows + width),
            transcendentals=0,
        ),
    )(normed, weight, bias.astype(F32)[None], cosine, sine)


def share(tiles, chip):
    at = (chip * tiles) // 8
    return at, ((chip + 1) * tiles) // 8 - at


def pack_kernel(tiles, part, gate_ref, up_ref, down_ref, both_out, down_out):
    at, count = share(tiles, pl.program_id(0))
    cols = pl.ds(pl.multiple_of(at * 128, 128), part)
    keep = lax.broadcasted_iota(jnp.int32, (gate_ref.shape[0], part), 1) < count * 128

    def kept(value):
        return jnp.where(keep, value.astype(F32), 0.0).astype(BF)

    both_out[0, :, :part] = kept(gate_ref[:, cols])
    both_out[0, :, part:] = kept(up_ref[:, cols])
    down_out[0] = kept(down_ref[:, cols])


def pack(w_gate, w_up, w_down, part):
    slab, hidden = w_gate.shape
    vmem = pl.BlockSpec(memory_space=pltpu.VMEM)
    return pl.pallas_call(
        functools.partial(pack_kernel, hidden // 128, part),
        grid=(8,),
        out_shape=(
            jax.ShapeDtypeStruct((8, slab, 2 * part), BF),
            jax.ShapeDtypeStruct((8, slab, part), BF),
        ),
        in_specs=[vmem] * 3,
        out_specs=(
            pl.BlockSpec((1, slab, 2 * part), lambda c: (c, 0, 0)),
            pl.BlockSpec((1, slab, part), lambda c: (c, 0, 0)),
        ),
        compiler_params=pltpu.CompilerParams(vmem_limit_bytes=24 * 2**20),
        cost_estimate=pl.CostEstimate(flops=0, bytes_accessed=8 * 2**20, transcendentals=0),
    )(w_gate, w_up, w_down)


def unpack_kernel(tiles, gate_ref, up_ref, down_ref, gate_out, up_out, down_out):
    for c in range(8):
        at, size = share(tiles, c)
        here, width = slice(at * 128, (at + size) * 128), size * 128
        gate_out[:, here] = gate_ref[c, :, :width].astype(F32)
        up_out[:, here] = up_ref[c, :, :width].astype(F32)
        down_out[:, here] = down_ref[c, :, :width].astype(F32)


def unpack(gate, up, down, hidden):
    slab = down.shape[1]
    vmem = pl.BlockSpec(memory_space=pltpu.VMEM)
    return pl.pallas_call(
        functools.partial(unpack_kernel, hidden // 128),
        out_shape=(
            jax.ShapeDtypeStruct((slab, hidden), F32),
            jax.ShapeDtypeStruct((slab, hidden), F32),
            jax.ShapeDtypeStruct((slab, hidden), F32),
        ),
        in_specs=[vmem] * 3,
        out_specs=(vmem,) * 3,
        compiler_params=pltpu.CompilerParams(vmem_limit_bytes=40 * 2**20),
        cost_estimate=pl.CostEstimate(flops=0, bytes_accessed=10 * 2**20, transcendentals=0),
    )(gate, up, down)


def shards(
    tokens,
    cotangent,
    norm_gain,
    w_query,
    b_query,
    w_key,
    b_key,
    w_value,
    b_value,
    w_out,
    ffn_gain,
    w_gate,
    w_up,
    w_down,
    unit_seq,
    block_map,
):
    rows, model = tokens.shape
    blocks = block_map.shape[0]
    low_rows = rows // 2
    width = w_query.shape[1]
    heads = width // HD
    slab = w_gate.shape[0]
    tiles = w_gate.shape[1] // 128
    part = -(-tiles // 8) * 128
    core = lax.axis_index("mp")
    me = lax.axis_index(BLK)

    def my_half(value):
        return halves(value.reshape((2, low_rows) + value.shape[1:]), core)

    bits = blocks.bit_length() - 1
    high = list(range(3, bits))[::-1]

    both_send, down_send = pack(w_gate, w_up, w_down.T, part)
    w_kv = Gather(jnp.concatenate([w_key, w_value], axis=1))
    w_q = Gather(w_query)
    w_out_all = Gather(w_out.T)
    cot_half = my_half(cotangent)
    cot_cube = Cube(cot_half)
    for bit in high:
        w_kv.step(bit)
        w_q.step(bit)
        w_out_all.step(bit)
    cot_cube.step(1)
    both_cube = trade(after(both_send, w_kv.last, w_q.last), CUBE_AXES)
    down_cube = trade(after(down_send, both_cube), CUBE_AXES)
    both_own = lax.all_gather(both_cube.reshape(8 * slab, -1), "h", axis=0, tiled=True)
    down_own = lax.all_gather(down_cube.reshape(8 * slab, -1), "h", axis=0, tiled=True)
    block_map = after(block_map, both_send)
    inputs = after(tokens, both_send).astype(F32)
    per_unit = SEG // rows
    units = jnp.arange(unit_seq.shape[0], dtype=jnp.int32)
    previous = jnp.concatenate([jnp.full((1,), -1, jnp.int32), unit_seq[:-1]])
    first_unit = lax.cummax(jnp.where(unit_seq != previous, units, 0), axis=0)
    seqs = look(unit_seq, block_map // per_unit)
    own_place = jnp.arange(blocks, dtype=jnp.int32) == me
    my_block = jnp.sum(jnp.where(own_place, block_map, 0))
    my_seq = jnp.sum(jnp.where(own_place, seqs, 0))
    vis = ((seqs == my_seq) & (block_map < my_block)).astype(jnp.int32)
    vis = jnp.concatenate([vis, me[None].astype(jnp.int32)])
    begin = look(first_unit, (my_block // per_unit)[None])
    position = my_block * rows - begin[0] * SEG + jnp.arange(rows, dtype=jnp.int32)
    cosine, sine = rope_tables(position)

    gain_one = norm_gain.astype(F32)
    inverse_one = lax.rsqrt(jnp.mean(inputs * inputs, axis=-1, keepdims=True) + epsilon)
    normed = (inputs * inverse_one * gain_one).astype(BF)
    w_kv.value = after(w_kv.value, both_cube, cosine, vis, normed)
    w_q.value = after(w_q.value, both_cube)
    w_kv.step(2)
    w_q.step(2)
    one, two = w_q.split(2)
    w_kv.step(1)
    one.step(0)
    two.step(1)
    cot_cube.value = after(cot_cube.value, w_q.last)
    cot_cube.step(2)
    w_kv = w_kv.step(0).rows()
    w_q = joined([one.step(1), two.step(0)]).rows()

    keyval = Gather(project(normed, w_kv, jnp.concatenate([b_key, b_value]), cosine, sine, 1))

    w_out_all.value = after(w_out_all.value, w_kv)
    for bit in high:
        keyval.step(bit)
    w_out_all.step(2)
    keyval.value = after(keyval.value, down_cube, w_out_all.last, cot_cube.last)
    keyval.step(2)
    w_out_all.step(0)
    key_part, value_part = keyval.split(2)
    key_part.value = after(key_part.value, w_out_all.last)
    key_part.step(0)
    value_part.step(1)
    key_part.step(1)
    value_part.step(0)
    w_out_all.value = after(w_out_all.value, key_part.last, value_part.last)
    cot_cube.value = after(cot_cube.value, key_part.last, value_part.last)
    keyval = joined([key_part, value_part]).value.reshape(blocks, rows, 2 * HD)
    out_full = w_out_all.step(1).rows()
    cot_cube.step(0)
    query = project(normed, w_q, b_query, cosine, sine, heads)
    attended, attended_low, lse = attend(vis, query, keyval)
    attended_low = after(attended_low, cot_cube.last)
    cot_cube = cot_cube.done()
    attn = dot(attended_low, out_full, NT).astype(BF).reshape(2, low_rows, model)
    attn = halves(attn, core).astype(F32) + swap_mp(halves(attn, 1 - core)).astype(F32)
    middle = my_half(tokens).astype(F32) + attn
    gain_two = ffn_gain.astype(F32)
    inverse_two = lax.rsqrt(jnp.mean(middle * middle, axis=-1, keepdims=True) + epsilon)
    normed_two = (middle * inverse_two * gain_two).astype(BF)
    cube_two, came = cube_gather(normed_two)
    both_own = after(both_own, *came)
    down_own = after(down_own, *came)
    both_w = (both_own, swap_mp(both_own))
    down_w = (down_own, swap_mp(down_own))

    def over_high_back(value):
        return lax.psum_scatter(value, "h", scatter_dimension=0, tiled=True)

    lins, hiddens, grads = [], [], []
    for both in both_w:
        lin = dot(cube_two, both)
        gate, up = lin[:, :part], lin[:, part:]
        sigmoid_gate = jax.nn.sigmoid(gate)
        silu_gate = gate * sigmoid_gate
        hiddens.append((silu_gate * up).astype(BF))
        lins.append((gate, up, sigmoid_gate, silu_gate))
    for (gate, up, sigmoid_gate, silu_gate), down in zip(lins, down_w):
        grad_hidden = dot(cot_cube, down)
        grad_gate = grad_hidden * up * sigmoid_gate * (1.0 + gate * (1.0 - sigmoid_gate))
        grad_up = grad_hidden * silu_gate
        grads.append(jnp.concatenate([grad_gate.astype(BF), grad_up.astype(BF)], axis=1))
    grad_two = dot(grads[0], both_w[0], NT) + dot(grads[1], both_w[1], NT)
    grad_two = grad_two.astype(BF)
    grads = [after(v, grad_two) for v in grads]
    hiddens = [after(v, grad_two) for v in hiddens]
    grad_two = CubeSum(grad_two, low_rows).step()
    gates, ups = [g[:, :part] for g in grads], [g[:, part:] for g in grads]
    theirs = [
        dot(cot_cube, hiddens[1], TN).astype(BF),
        dot(cube_two, gates[1], TN).astype(BF),
        dot(cube_two, ups[1], TN).astype(BF),
    ]
    came = [swap_mp(v) for v in theirs]
    grad_two.step(*theirs)
    down_back = (dot(cot_cube, hiddens[0], TN) + came[0].astype(F32)).astype(BF)
    down_high = over_high_back(down_back)
    gate_back = (dot(cube_two, gates[0], TN) + came[1].astype(F32)).astype(BF)
    gate_high = over_high_back(gate_back)
    grad_two.step(down_back, gate_back)
    up_back = (dot(cube_two, ups[0], TN) + came[2].astype(F32)).astype(BF)
    up_high = over_high_back(up_back)
    grad_two = after(grad_two.total(), up_back)

    def whole(own):
        other = swap_mp(own)
        return jnp.where(
            core == 0, jnp.concatenate([own, other], 0), jnp.concatenate([other, own], 0)
        )

    grad_middle_norm, grad_gain_two = norm_back(grad_two, middle, inverse_two, gain_two)
    grad_middle_half = cot_half.astype(F32) + grad_middle_norm
    grad_attn = whole(grad_middle_half.astype(BF))
    grad_middle = whole(grad_middle_half)
    grad_attended = dot(grad_attn, out_full).astype(BF)
    out_grad = dot(grad_attn, attended_low, TN).astype(BF)
    grad_q, grad_kv_all = attend_back(
        vis, query, keyval, grad_attended, attended, lse, cosine, sine
    )
    low = [2] + high[::-1]

    def pair(grad):
        n = grad.shape[1] // 2
        return [Scatter(grad[:, :n], bits), Scatter(grad[:, n:], bits)]

    def merge(parts):
        parts[0].value = jnp.concatenate([p.value for p in parts], axis=-1)
        return parts[0]

    def hold(parts, *others):
        for p in parts:
            p.value = after(p.value, *others)

    def home(value, *others):
        return trade(after(value, *others).reshape(8, slab, part), CUBE_AXES)

    out_sum = pair(out_grad)
    out_sum[0].step(0)
    out_sum[1].step(1)
    kv_sum = pair(grad_kv_all.reshape(blocks * rows, 2 * HD))
    hold(kv_sum, out_sum[0].last, out_sum[1].last)
    kv_sum[0].step(0)
    kv_sum[1].step(1)
    hiddens = [after(v, kv_sum[0].last) for v in hiddens]
    ffn = (dot(hiddens[0], down_w[0], NT) + dot(hiddens[1], down_w[1], NT)).astype(BF)
    query_grad = dot(normed, after(grad_q, kv_sum[0].last), TN).astype(BF)
    kv_sum[0].step(1)
    kv_sum[1].step(0)
    hold(out_sum, kv_sum[0].last, kv_sum[1].last)
    kv_sum = merge(kv_sum)
    kv_sum.step(2)
    hold(out_sum, kv_sum.last)
    query_sum = pair(query_grad)
    hold(query_sum, kv_sum.last)
    out_sum[0].step(1)
    out_sum[1].step(0)
    query_sum[0].step(0)
    query_sum[1].step(1)
    down_back = home(down_high, kv_sum.last)
    ffn = CubeSum(ffn, low_rows)
    for bit in high[::-1]:
        kv_sum.step(bit)
    out_sum = merge(out_sum)
    hold([out_sum], kv_sum.last)
    grad_k = rotate(kv_sum.value[:, :HD], cosine, -sine).astype(BF)
    grad_v = kv_sum.value[:, HD:].astype(BF)
    grad_kv = jnp.concatenate([grad_k, grad_v], axis=1)
    last = Scatter(dot(normed, grad_kv, TN).astype(BF), bits)
    last.step(1)
    grad_normed = (dot(grad_q, w_q, NT) + dot(grad_kv, w_kv, NT)).astype(BF)
    other_normed = swap_mp(grad_normed)
    hold([last], other_normed, query_sum[0].last, query_sum[1].last)
    last.step(0)
    hold([out_sum], last.last)
    hold(query_sum, last.last)
    query_sum[0].step(1)
    query_sum[1].step(0)
    query_sum = merge(query_sum)
    last.step(2)
    hold([out_sum], last.last)
    hold([query_sum], last.last)
    for bit in high[::-1]:
        last.step(bit)
    gate_back = home(gate_high, down_back, last.last)
    out_sum.step(2)
    query_sum.step(2)
    grad_normed = grad_normed.astype(F32) + other_normed.astype(F32)
    grad_input_norm, grad_gain_one = norm_back(grad_normed, inputs, inverse_one, gain_one)
    grad_tokens = grad_middle + grad_input_norm
    bias_query = jnp.sum(grad_q.astype(F32), axis=0)
    bias_kv = jnp.sum(grad_kv.astype(F32), axis=0)
    gain_two_sum = grad_gain_two + swap_mp(grad_gain_two)
    small = jnp.concatenate([grad_gain_one, gain_two_sum, bias_query, bias_kv]).reshape(-1, 128)
    came = flip(after(small, last.last), 0)
    small = small + came
    hold([out_sum], query_sum.last, came)
    hold([query_sum], out_sum.last, came)
    ffn.step(last.last)
    for bit in high[::-1]:
        out_sum.step(bit)
        query_sum.step(bit)
    came = flip(after(small, out_sum.last, query_sum.last), 1)
    small = small + came
    up_back = home(up_high, gate_back, *ffn.came)
    ffn.step(came)
    small = small + flip(after(small, *ffn.came), 2)
    for bit in high:
        small = small + flip(small, bit)
    ffn.step()
    mixed = whole((middle + ffn.total()).astype(BF))
    small = small.reshape(-1)
    out_part, query_part, kv_part = out_sum.value, query_sum.value, last.value

    gate_part, up_part, down_part = unpack(gate_back, up_back, down_back, w_gate.shape[1])
    gain_one_sum = small[:model]
    gain_two_sum = small[model : 2 * model]
    bias_query_sum = small[2 * model : 2 * model + width]
    bias_key_sum = small[2 * model + width : 2 * model + width + HD]
    bias_value_sum = small[2 * model + width + HD :]
    return (
        mixed,
        grad_tokens,
        gain_one_sum,
        query_part,
        bias_query_sum,
        kv_part[:, :HD],
        bias_key_sum,
        kv_part[:, HD:],
        bias_value_sum,
        out_part.T,
        gain_two_sum,
        gate_part,
        up_part,
        down_part.T,
    )


def solution(mesh):
    blocks, cores = mesh.devices.shape
    mesh = Mesh(
        mesh.devices.reshape(blocks // 8, 2, 2, 2, cores), ("h", "a", "y", "x", "mp")
    )
    blk = ("h", "a", "y", "x")
    placed = (
        P(blk, None),
        P(blk, None),
        P(),
        P(blk, "mp"),
        P("mp"),
        P(blk, "mp"),
        P("mp"),
        P(blk, "mp"),
        P("mp"),
        P("mp", blk),
        P(),
        P(blk, "mp"),
        P(blk, "mp"),
        P("mp", blk),
        P(),
        P(),
    )
    return jax.shard_map(
        shards,
        mesh=mesh,
        in_specs=placed,
        out_specs=(
            P(blk, None),
            P(blk, None),
            P(),
            P(blk, "mp"),
            P("mp"),
            P(blk, "mp"),
            P("mp"),
            P(blk, "mp"),
            P("mp"),
            P("mp", blk),
            P(),
            P(blk, "mp"),
            P(blk, "mp"),
            P("mp", blk),
        ),
        check_vma=False,
    )
```

```python
import functools

import jax
import jax.numpy as jnp
from jax import lax
from jax.experimental import pallas as pl
from jax.experimental.pallas import tpu as pltpu
from jax.sharding import Mesh
from jax.sharding import PartitionSpec as P

HD = 128
SEG = 1024
LOG2E = 1.4426950408889634
BIG = -1e30
BF = jnp.bfloat16
F32 = jnp.float32

epsilon = 1e-06


BLK = ("h", "a", "y", "x")
CUBE_AXES = ("a", "y", "x")


def bit_axis(bit):
    return ("x", "y", "a")[bit] if bit < 3 else "h", 1 if bit < 3 else 1 << (bit - 3)


def flip(value, bit):
    axis, mask = bit_axis(bit)
    return lax.ppermute(value, axis, [(i, i ^ mask) for i in range(lax.axis_size(axis))])


def mine(bit):
    axis, mask = bit_axis(bit)
    return (lax.axis_index(axis) // mask) % 2


def swap_mp(value):
    return lax.ppermute(value, "mp", [(0, 1), (1, 0)])


def halves(value, which):
    return lax.dynamic_index_in_dim(value, which, 0, keepdims=False)


def trade(value, axes, dim=0):
    return lax.all_to_all(value, axes, dim, dim, tiled=True)


def after(value, *others):
    if not others:
        return value
    return lax.optimization_barrier((value,) + others)[0]


def together(values):
    return list(lax.optimization_barrier(tuple(values)))


class Gather:
    def __init__(self, value):
        self.value, self.have = value, []

    def step(self, bit):
        at = sum(1 for b in self.have if b > bit)
        other = flip(self.value, bit)
        self.last = other
        self.value = jnp.where(
            mine(bit) == 0,
            jnp.stack([self.value, other], at),
            jnp.stack([other, self.value], at),
        )
        self.have.append(bit)
        return self

    def split(self, count):
        parts = []
        for value in jnp.split(self.value, count, axis=-1):
            part = Gather(value)
            part.have = list(self.have)
            parts.append(part)
        return parts

    def rows(self):
        return self.value.reshape((-1, self.value.shape[-1]))


class Scatter:
    def __init__(self, value, bits):
        self.have = list(range(bits))[::-1]
        self.value = value.reshape((2,) * bits + (-1, value.shape[-1]))

    def step(self, bit, *others):
        at = self.have.index(bit)
        me = mine(bit)
        keep = lax.dynamic_index_in_dim(self.value, me, at, keepdims=False)
        send = lax.dynamic_index_in_dim(self.value, 1 - me, at, keepdims=False)
        self.last = flip(send, bit)
        if others:
            self.last = after(self.last, *others)
        self.value = keep.astype(F32) + self.last.astype(F32)
        self.have.remove(bit)
        if self.have:
            self.value = self.value.astype(BF)
        return self


def joined(parts):
    one = Gather(jnp.concatenate([p.value for p in parts], axis=-1))
    one.have = list(parts[0].have)
    return one


CUBE = ((0, 1, 2), (1, 2, 0), (2, 0, 1))


def cube_parts(rows):
    units = rows // 8
    sizes = [(units + 2 - i) // 3 * 8 for i in range(3)]
    return sizes


def cube_gather(value):
    parts, at = [], 0
    for size in cube_parts(value.shape[0]):
        parts.append(value[at : at + size])
        at += size
    for step in range(3):
        came = together([flip(part, order[step]) for part, order in zip(parts, CUBE)])
        parts = [jnp.concatenate(both, 0) for both in zip(parts, came)]
    return jnp.concatenate(parts, 0), came


class Cube:
    def __init__(self, value):
        self.value, self.size, self.have = value, value.shape[0], [0]

    def step(self, bit):
        self.last = flip(self.value, bit)
        self.value = jnp.concatenate([self.value, self.last], 0)
        self.have = self.have + [h ^ (1 << bit) for h in self.have]
        return self

    def done(self):
        slots = self.value.reshape((8, self.size) + self.value.shape[1:])
        pieces, at = [], 0
        for rows, order in zip(cube_parts(self.size), CUBE):
            wanted = [0]
            for bit in order:
                wanted = wanted + [w ^ (1 << bit) for w in wanted]
            pieces += [slots[self.have.index(w), at : at + rows] for w in wanted]
            at += rows
        return jnp.concatenate(pieces, 0)


class CubeSum:
    def __init__(self, value, rows):
        self.parts, self.number, at = [], 0, 0
        for size in cube_parts(rows):
            self.parts.append(value[at : at + 8 * size])
            at += 8 * size

    def step(self, *others):
        half = [part.shape[0] // 2 for part in self.parts]
        sent = [
            flip(after(p[n:], *others), order[2 - self.number])
            for p, n, order in zip(self.parts, half, CUBE)
        ]
        self.came = together(sent)
        self.parts = [
            p[:n].astype(F32) + v.astype(F32) for p, n, v in zip(self.parts, half, self.came)
        ]
        self.number += 1
        if self.number < 3:
            self.parts = [p.astype(BF) for p in self.parts]
        return self

    def total(self):
        return jnp.concatenate(self.parts, 0)


def rotate(value, cosine, sine):
    half = value.shape[-1] // 2
    return value * cosine + jnp.concatenate([value[:, half:], value[:, :half]], axis=1) * sine


def rope_tables(position):
    freq = jnp.power(10000.0, -(jnp.arange(HD // 2, dtype=F32) * (2.0 / HD)))
    angle = position.astype(F32)[:, None] * freq[None, :]
    cosine, sine = jnp.cos(angle), jnp.sin(angle)
    return (jnp.concatenate([cosine, cosine], 1), jnp.concatenate([-sine, sine], 1))


def look(table, index):
    places = jnp.arange(table.shape[0], dtype=jnp.int32)
    return jnp.sum(jnp.where(index[:, None] == places[None, :], table[None, :], 0), axis=1)


def norm_back(grad, value, inverse, gain):
    scaled = grad * gain
    grad_gain = jnp.sum(grad * value * inverse, axis=0)
    mean_term = jnp.mean(scaled * value, axis=-1, keepdims=True)
    grad_value = inverse * scaled - value * (inverse * inverse * inverse) * mean_term
    return (grad_value, grad_gain)


NT = (((1,), (1,)), ((), ()))
TN = (((0,), (0,)), ((), ()))


def dot(left, right, dims=(((1,), (0,)), ((), ()))):
    return lax.dot_general(left, right, dims, preferred_element_type=F32)


def attend_kernel(vis, q_ref, kv_ref, o_ref, low_ref, lse_ref, acc, top, tot):
    rows, width = q_ref.shape
    heads = width // HD
    blocks = kv_ref.shape[0]
    factor = HD ** (-0.5) * LOG2E

    def block(place, first):
        key = kv_ref[place, :, :HD]
        value = kv_ref[place, :, HD:].astype(F32).T.astype(BF)
        if first:
            mask = lax.broadcasted_iota(jnp.int32, (rows, rows), 0) <= lax.broadcasted_iota(
                jnp.int32, (rows, rows), 1
            )
        for h in range(heads):
            scores = dot(key, q_ref[:, h * HD : (h + 1) * HD], NT) * factor
            if first:
                scores = jnp.where(mask, scores, BIG)
                best = jnp.max(scores, axis=0, keepdims=True)
                weights = jnp.exp2(scores - best)
                tot[h] = jnp.sum(weights, axis=0, keepdims=True)
                acc[h] = dot(value, weights.astype(BF))
            else:
                old = top[h]
                best = jnp.maximum(old, jnp.max(scores, axis=0, keepdims=True))
                weights = jnp.exp2(scores - best)
                scale = jnp.exp2(old - best)
                tot[h] = tot[h] * scale + jnp.sum(weights, axis=0, keepdims=True)
                acc[h] = acc[h] * scale + dot(value, weights.astype(BF))
            top[h] = best

    block(vis[blocks], True)

    def step(place, carry):
        @pl.when(vis[place] == 1)
        def _():
            block(place, False)

        return carry

    lax.fori_loop(0, blocks, step, 0)
    for h in range(heads):
        cols = slice(h * HD, (h + 1) * HD)
        total = tot[h]
        out = (acc[h] / total).T
        o_ref[:, cols] = out
        low_ref[:, cols] = out.astype(BF)
        lse_ref[h] = top[h] + jnp.log(total) * LOG2E


def attend(vis, query, keyval):
    rows, width = query.shape
    heads = width // HD
    smem = pl.BlockSpec(memory_space=pltpu.SMEM)
    vmem = pl.BlockSpec(memory_space=pltpu.VMEM)
    return pl.pallas_call(
        attend_kernel,
        out_shape=(
            jax.ShapeDtypeStruct((rows, width), F32),
            jax.ShapeDtypeStruct((rows, width), BF),
            jax.ShapeDtypeStruct((heads, 1, rows), F32),
        ),
        in_specs=[smem, vmem, vmem],
        out_specs=(vmem, vmem, vmem),
        scratch_shapes=[
            pltpu.VMEM((heads, HD, rows), F32),
            pltpu.VMEM((heads, 1, rows), F32),
            pltpu.VMEM((heads, 1, rows), F32),
        ],
        compiler_params=pltpu.CompilerParams(vmem_limit_bytes=40 * 2**20),
        cost_estimate=pl.CostEstimate(
            flops=4 * rows * width * 2048, bytes_accessed=8 * 2**20, transcendentals=rows * 6 * 2048
        ),
    )(vis, query, keyval)


def attend_back_kernel(
    vis, q_ref, kv_ref, do_ref, o_ref, lse_ref, cos_ref, sin_ref, out_ref, dkv_ref, dq_ref, delta
):
    rows, width = q_ref.shape
    heads = width // HD
    blocks = kv_ref.shape[0]
    scale = HD ** (-0.5)
    for h in range(heads):
        cols = slice(h * HD, (h + 1) * HD)
        product = (do_ref[:, cols].astype(F32) * o_ref[:, cols]).T
        delta[h] = jnp.sum(product, axis=0, keepdims=True)

    def block(place, first):
        key = kv_ref[place, :, :HD]
        value = kv_ref[place, :, HD:]
        if first:
            mask = lax.broadcasted_iota(jnp.int32, (rows, rows), 0) <= lax.broadcasted_iota(
                jnp.int32, (rows, rows), 1
            )
        dk = jnp.zeros((rows, HD), F32)
        dv = jnp.zeros((rows, HD), F32)
        for h in range(heads):
            cols = slice(h * HD, (h + 1) * HD)
            query = q_ref[:, cols]
            grad = do_ref[:, cols]
            probs = jnp.exp2(dot(key, query, NT) * (scale * LOG2E) - lse_ref[h])
            if first:
                probs = jnp.where(mask, probs, 0.0)
            dv = dv + dot(probs.astype(BF), grad)
            dprobs = dot(value, grad, NT)
            dscores = (probs * (dprobs - delta[h])).astype(BF)
            dk = dk + dot(dscores, query)
            dq = dot(dscores, key, TN) * scale
            if first:
                dq_ref[:, cols] = dq
            else:
                dq_ref[:, cols] = dq_ref[:, cols] + dq
        dkv_ref[place, :, :HD] = (dk * scale).astype(BF)
        dkv_ref[place, :, HD:] = dv.astype(BF)

    block(vis[blocks], True)

    def step(place, carry):
        @pl.when(vis[place] == 1)
        def _():
            block(place, False)

        @pl.when((vis[place] == 0) & (place != vis[blocks]))
        def _():
            dkv_ref[place] = jnp.zeros((rows, 2 * HD), BF)

        return carry

    lax.fori_loop(0, blocks, step, 0)
    for h in range(heads):
        cols = slice(h * HD, (h + 1) * HD)
        out_ref[:, cols] = turn(dq_ref[:, cols], cos_ref[...], -sin_ref[...]).astype(BF)


def attend_back(vis, query, keyval, grad, out, lse, cosine, sine):
    rows, width = query.shape
    heads = width // HD
    smem = pl.BlockSpec(memory_space=pltpu.SMEM)
    vmem = pl.BlockSpec(memory_space=pltpu.VMEM)
    return pl.pallas_call(
        attend_back_kernel,
        out_shape=(
            jax.ShapeDtypeStruct((rows, width), BF),
            jax.ShapeDtypeStruct(keyval.shape, BF),
        ),
        in_specs=[smem] + [vmem] * 7,
        out_specs=(vmem, vmem),
        scratch_shapes=[
            pltpu.VMEM((rows, width), F32),
            pltpu.VMEM((heads, 1, rows), F32),
        ],
        compiler_params=pltpu.CompilerParams(vmem_limit_bytes=48 * 2**20),
        cost_estimate=pl.CostEstimate(
            flops=10 * rows * width * 2048,
            bytes_accessed=16 * 2**20,
            transcendentals=rows * 6 * 2048,
        ),
    )(vis, query, keyval, grad, out, lse, cosine, sine)


def turn(value, cosine, sine):
    return value * cosine + pltpu.roll(value, HD // 2, 1) * sine


def project_kernel(turned, x_ref, w_ref, b_ref, cos_ref, sin_ref, o_ref):
    lin = dot(x_ref[...], w_ref[...]) + b_ref[...]
    for h in range(lin.shape[1] // HD):
        cols = slice(h * HD, (h + 1) * HD)
        head = lin[:, cols]
        if h < turned:
            head = turn(head, cos_ref[...], sin_ref[...])
        o_ref[:, cols] = head.astype(BF)


def project(normed, weight, bias, cosine, sine, turned):
    rows = normed.shape[0]
    width = weight.shape[1]
    vmem = pl.BlockSpec(memory_space=pltpu.VMEM)
    return pl.pallas_call(
        functools.partial(project_kernel, turned),
        out_shape=jax.ShapeDtypeStruct((rows, width), BF),
        in_specs=[vmem] * 5,
        out_specs=vmem,
        compiler_params=pltpu.CompilerParams(vmem_limit_bytes=24 * 2**20),
        cost_estimate=pl.CostEstimate(
            flops=2 * rows * width * normed.shape[1],
            bytes_accessed=2 * normed.shape[1] * (rows + width),
            transcendentals=0,
        ),
    )(normed, weight, bias.astype(F32)[None], cosine, sine)


def share(tiles, chip):
    at = (chip * tiles) // 8
    return at, ((chip + 1) * tiles) // 8 - at


def pack_kernel(tiles, part, gate_ref, up_ref, down_ref, both_out, down_out):
    at, count = share(tiles, pl.program_id(0))
    cols = pl.ds(pl.multiple_of(at * 128, 128), part)
    keep = lax.broadcasted_iota(jnp.int32, (gate_ref.shape[0], part), 1) < count * 128

    def kept(value):
        return jnp.where(keep, value.astype(F32), 0.0).astype(BF)

    both_out[0, :, :part] = kept(gate_ref[:, cols])
    both_out[0, :, part:] = kept(up_ref[:, cols])
    down_out[0] = kept(down_ref[:, cols])


def pack(w_gate, w_up, w_down, part):
    slab, hidden = w_gate.shape
    vmem = pl.BlockSpec(memory_space=pltpu.VMEM)
    return pl.pallas_call(
        functools.partial(pack_kernel, hidden // 128, part),
        grid=(8,),
        out_shape=(
            jax.ShapeDtypeStruct((8, slab, 2 * part), BF),
            jax.ShapeDtypeStruct((8, slab, part), BF),
        ),
        in_specs=[vmem] * 3,
        out_specs=(
            pl.BlockSpec((1, slab, 2 * part), lambda c: (c, 0, 0)),
            pl.BlockSpec((1, slab, part), lambda c: (c, 0, 0)),
        ),
        compiler_params=pltpu.CompilerParams(vmem_limit_bytes=24 * 2**20),
        cost_estimate=pl.CostEstimate(flops=0, bytes_accessed=8 * 2**20, transcendentals=0),
    )(w_gate, w_up, w_down)


def unpack_kernel(tiles, gate_ref, up_ref, down_ref, gate_out, up_out, down_out):
    for c in range(8):
        at, size = share(tiles, c)
        here, width = slice(at * 128, (at + size) * 128), size * 128
        gate_out[:, here] = gate_ref[c, :, :width].astype(F32)
        up_out[:, here] = up_ref[c, :, :width].astype(F32)
        down_out[:, here] = down_ref[c, :, :width].astype(F32)


def unpack(gate, up, down, hidden):
    slab = down.shape[1]
    vmem = pl.BlockSpec(memory_space=pltpu.VMEM)
    return pl.pallas_call(
        functools.partial(unpack_kernel, hidden // 128),
        out_shape=(
            jax.ShapeDtypeStruct((slab, hidden), F32),
            jax.ShapeDtypeStruct((slab, hidden), F32),
            jax.ShapeDtypeStruct((slab, hidden), F32),
        ),
        in_specs=[vmem] * 3,
        out_specs=(vmem,) * 3,
        compiler_params=pltpu.CompilerParams(vmem_limit_bytes=40 * 2**20),
        cost_estimate=pl.CostEstimate(flops=0, bytes_accessed=10 * 2**20, transcendentals=0),
    )(gate, up, down)


def shards(
    tokens,
    cotangent,
    norm_gain,
    w_query,
    b_query,
    w_key,
    b_key,
    w_value,
    b_value,
    w_out,
    ffn_gain,
    w_gate,
    w_up,
    w_down,
    unit_seq,
    block_map,
):
    rows, model = tokens.shape
    blocks = block_map.shape[0]
    low_rows = rows // 2
    width = w_query.shape[1]
    heads = width // HD
    slab = w_gate.shape[0]
    tiles = w_gate.shape[1] // 128
    part = -(-tiles // 8) * 128
    core = lax.axis_index("mp")
    me = lax.axis_index(BLK)

    def my_half(value):
        return halves(value.reshape((2, low_rows) + value.shape[1:]), core)

    bits = blocks.bit_length() - 1
    high = list(range(3, bits))[::-1]

    both_send, down_send = pack(w_gate, w_up, w_down.T, part)
    w_kv = Gather(jnp.concatenate([w_key, w_value], axis=1))
    w_q = Gather(w_query)
    w_out_all = Gather(w_out.T)
    cot_half = my_half(cotangent)
    cot_cube = Cube(cot_half)
    for bit in high:
        w_kv.step(bit)
        w_q.step(bit)
        w_out_all.step(bit)
    cot_cube.step(1)
    both_cube = trade(after(both_send, w_kv.last, w_q.last), CUBE_AXES)
    down_cube = trade(after(down_send, both_cube), CUBE_AXES)
    both_own = lax.all_gather(both_cube.reshape(8 * slab, -1), "h", axis=0, tiled=True)
    down_own = lax.all_gather(down_cube.reshape(8 * slab, -1), "h", axis=0, tiled=True)
    block_map = after(block_map, both_send)
    inputs = after(tokens, both_send).astype(F32)
    per_unit = SEG // rows
    units = jnp.arange(unit_seq.shape[0], dtype=jnp.int32)
    previous = jnp.concatenate([jnp.full((1,), -1, jnp.int32), unit_seq[:-1]])
    first_unit = lax.cummax(jnp.where(unit_seq != previous, units, 0), axis=0)
    seqs = look(unit_seq, block_map // per_unit)
    own_place = jnp.arange(blocks, dtype=jnp.int32) == me
    my_block = jnp.sum(jnp.where(own_place, block_map, 0))
    my_seq = jnp.sum(jnp.where(own_place, seqs, 0))
    vis = ((seqs == my_seq) & (block_map < my_block)).astype(jnp.int32)
    vis = jnp.concatenate([vis, me[None].astype(jnp.int32)])
    begin = look(first_unit, (my_block // per_unit)[None])
    position = my_block * rows - begin[0] * SEG + jnp.arange(rows, dtype=jnp.int32)
    cosine, sine = rope_tables(position)

    gain_one = norm_gain.astype(F32)
    inverse_one = lax.rsqrt(jnp.mean(inputs * inputs, axis=-1, keepdims=True) + epsilon)
    normed = (inputs * inverse_one * gain_one).astype(BF)
    w_kv.value = after(w_kv.value, both_cube, cosine, vis, normed)
    w_q.value = after(w_q.value, both_cube)
    w_kv.step(2)
    w_q.step(2)
    one, two = w_q.split(2)
    w_kv.step(1)
    one.step(0)
    two.step(1)
    cot_cube.value = after(cot_cube.value, w_q.last)
    cot_cube.step(2)
    w_kv = w_kv.step(0).rows()
    w_q = joined([one.step(1), two.step(0)]).rows()

    keyval = Gather(project(normed, w_kv, jnp.concatenate([b_key, b_value]), cosine, sine, 1))

    w_out_all.value = after(w_out_all.value, w_kv)
    for bit in high:
        keyval.step(bit)
    w_out_all.step(2)
    keyval.value = after(keyval.value, down_cube, w_out_all.last, cot_cube.last)
    keyval.step(2)
    w_out_all.step(0)
    key_part, value_part = keyval.split(2)
    key_part.value = after(key_part.value, w_out_all.last)
    key_part.step(0)
    value_part.step(1)
    key_part.step(1)
    value_part.step(0)
    w_out_all.value = after(w_out_all.value, key_part.last, value_part.last)
    cot_cube.value = after(cot_cube.value, key_part.last, value_part.last)
    keyval = joined([key_part, value_part]).value.reshape(blocks, rows, 2 * HD)
    out_full = w_out_all.step(1).rows()
    cot_cube.step(0)
    query = project(normed, w_q, b_query, cosine, sine, heads)
    attended, attended_low, lse = attend(vis, query, keyval)
    attended_low = after(attended_low, cot_cube.last)
    cot_cube = cot_cube.done()
    attn = dot(attended_low, out_full, NT).astype(BF).reshape(2, low_rows, model)
    attn = halves(attn, core).astype(F32) + swap_mp(halves(attn, 1 - core)).astype(F32)
    middle = my_half(tokens).astype(F32) + attn
    gain_two = ffn_gain.astype(F32)
    inverse_two = lax.rsqrt(jnp.mean(middle * middle, axis=-1, keepdims=True) + epsilon)
    normed_two = (middle * inverse_two * gain_two).astype(BF)
    cube_two, came = cube_gather(normed_two)
    both_own = after(both_own, *came)
    down_own = after(down_own, *came)
    both_w = (both_own, swap_mp(both_own))
    down_w = (down_own, swap_mp(down_own))

    def over_high_back(value):
        return lax.psum_scatter(value, "h", scatter_dimension=0, tiled=True)

    lins, hiddens, grads = [], [], []
    for both in both_w:
        lin = dot(cube_two, both)
        gate, up = lin[:, :part], lin[:, part:]
        sigmoid_gate = jax.nn.sigmoid(gate)
        silu_gate = gate * sigmoid_gate
        hiddens.append((silu_gate * up).astype(BF))
        lins.append((gate, up, sigmoid_gate, silu_gate))
    for (gate, up, sigmoid_gate, silu_gate), down in zip(lins, down_w):
        grad_hidden = dot(cot_cube, down)
        grad_gate = grad_hidden * up * sigmoid_gate * (1.0 + gate * (1.0 - sigmoid_gate))
        grad_up = grad_hidden * silu_gate
        grads.append(jnp.concatenate([grad_gate.astype(BF), grad_up.astype(BF)], axis=1))
    grad_two = dot(grads[0], both_w[0], NT) + dot(grads[1], both_w[1], NT)
    grad_two = grad_two.astype(BF)
    grads = [after(v, grad_two) for v in grads]
    hiddens = [after(v, grad_two) for v in hiddens]
    grad_two = CubeSum(grad_two, low_rows).step()
    gates, ups = [g[:, :part] for g in grads], [g[:, part:] for g in grads]
    theirs = [
        dot(cot_cube, hiddens[1], TN).astype(BF),
        dot(cube_two, gates[1], TN).astype(BF),
        dot(cube_two, ups[1], TN).astype(BF),
    ]
    came = [swap_mp(v) for v in theirs]
    grad_two.step(*theirs)
    down_back = (dot(cot_cube, hiddens[0], TN) + came[0].astype(F32)).astype(BF)
    down_high = over_high_back(down_back)
    gate_back = (dot(cube_two, gates[0], TN) + came[1].astype(F32)).astype(BF)
    gate_high = over_high_back(gate_back)
    grad_two.step(down_back, gate_back)
    up_back = (dot(cube_two, ups[0], TN) + came[2].astype(F32)).astype(BF)
    up_high = over_high_back(up_back)
    grad_two = after(grad_two.total(), up_back)

    def whole(own):
        other = swap_mp(own)
        return jnp.where(
            core == 0, jnp.concatenate([own, other], 0), jnp.concatenate([other, own], 0)
        )

    grad_middle_norm, grad_gain_two = norm_back(grad_two, middle, inverse_two, gain_two)
    grad_middle_half = cot_half.astype(F32) + grad_middle_norm
    grad_attn = whole(grad_middle_half.astype(BF))
    grad_middle = whole(grad_middle_half)
    grad_attended = dot(grad_attn, out_full).astype(BF)
    out_grad = dot(grad_attn, attended_low, TN).astype(BF)
    grad_q, grad_kv_all = attend_back(
        vis, query, keyval, grad_attended, attended, lse, cosine, sine
    )
    low = [2] + high[::-1]

    def pair(grad):
        n = grad.shape[1] // 2
        return [Scatter(grad[:, :n], bits), Scatter(grad[:, n:], bits)]

    def merge(parts):
        parts[0].value = jnp.concatenate([p.value for p in parts], axis=-1)
        return parts[0]

    def hold(parts, *others):
        for p in parts:
            p.value = after(p.value, *others)

    def home(value, *others):
        return trade(after(value, *others).reshape(8, slab, part), CUBE_AXES)

    out_sum = pair(out_grad)
    out_sum[0].step(0)
    out_sum[1].step(1)
    kv_sum = pair(grad_kv_all.reshape(blocks * rows, 2 * HD))
    hold(kv_sum, out_sum[0].last, out_sum[1].last)
    kv_sum[0].step(0)
    kv_sum[1].step(1)
    hiddens = [after(v, kv_sum[0].last) for v in hiddens]
    ffn = (dot(hiddens[0], down_w[0], NT) + dot(hiddens[1], down_w[1], NT)).astype(BF)
    query_grad = dot(normed, after(grad_q, kv_sum[0].last), TN).astype(BF)
    kv_sum[0].step(1)
    kv_sum[1].step(0)
    hold(out_sum, kv_sum[0].last, kv_sum[1].last)
    kv_sum = merge(kv_sum)
    kv_sum.step(2)
    hold(out_sum, kv_sum.last)
    query_sum = pair(query_grad)
    hold(query_sum, kv_sum.last)
    out_sum[0].step(1)
    out_sum[1].step(0)
    query_sum[0].step(0)
    query_sum[1].step(1)
    down_back = home(down_high, kv_sum.last)
    ffn = CubeSum(ffn, low_rows)
    for bit in high[::-1]:
        kv_sum.step(bit)
    out_sum = merge(out_sum)
    hold([out_sum], kv_sum.last)
    grad_k = rotate(kv_sum.value[:, :HD], cosine, -sine).astype(BF)
    grad_v = kv_sum.value[:, HD:].astype(BF)
    grad_kv = jnp.concatenate([grad_k, grad_v], axis=1)
    last = Scatter(dot(normed, grad_kv, TN).astype(BF), bits)
    last.step(1)
    grad_normed = (dot(grad_q, w_q, NT) + dot(grad_kv, w_kv, NT)).astype(BF)
    other_normed = swap_mp(grad_normed)
    hold([last], other_normed, query_sum[0].last, query_sum[1].last)
    last.step(0)
    hold([out_sum], last.last)
    hold(query_sum, last.last)
    query_sum[0].step(1)
    query_sum[1].step(0)
    query_sum = merge(query_sum)
    last.step(2)
    hold([out_sum], last.last)
    hold([query_sum], last.last)
    for bit in high[::-1]:
        last.step(bit)
    gate_back = home(gate_high, down_back, last.last)
    out_sum.step(2)
    query_sum.step(2)
    grad_normed = grad_normed.astype(F32) + other_normed.astype(F32)
    grad_input_norm, grad_gain_one = norm_back(grad_normed, inputs, inverse_one, gain_one)
    grad_tokens = grad_middle + grad_input_norm
    bias_query = jnp.sum(grad_q.astype(F32), axis=0)
    bias_kv = jnp.sum(grad_kv.astype(F32), axis=0)
    gain_two_sum = grad_gain_two + swap_mp(grad_gain_two)
    small = jnp.concatenate([grad_gain_one, gain_two_sum, bias_query, bias_kv]).reshape(-1, 128)
    came = flip(after(small, last.last), 0)
    small = small + came
    hold([out_sum], query_sum.last, came)
    hold([query_sum], out_sum.last, came)
    ffn.step(last.last)
    for bit in high[::-1]:
        out_sum.step(bit)
        query_sum.step(bit)
    came = flip(after(small, out_sum.last, query_sum.last), 1)
    small = small + came
    up_back = home(up_high, gate_back, *ffn.came)
    ffn.step(came)
    small = small + flip(after(small, *ffn.came), 2)
    for bit in high:
        small = small + flip(small, bit)
    ffn.step()
    mixed = whole((middle + ffn.total()).astype(BF))
    small = small.reshape(-1)
    out_part, query_part, kv_part = out_sum.value, query_sum.value, last.value

    gate_part, up_part, down_part = unpack(gate_back, up_back, down_back, w_gate.shape[1])
    gain_one_sum = small[:model]
    gain_two_sum = small[model : 2 * model]
    bias_query_sum = small[2 * model : 2 * model + width]
    bias_key_sum = small[2 * model + width : 2 * model + width + HD]
    bias_value_sum = small[2 * model + width + HD :]
    return (
        mixed,
        grad_tokens,
        gain_one_sum,
        query_part,
        bias_query_sum,
        kv_part[:, :HD],
        bias_key_sum,
        kv_part[:, HD:],
        bias_value_sum,
        out_part.T,
        gain_two_sum,
        gate_part,
        up_part,
        down_part.T,
    )


def solution(mesh):
    blocks, cores = mesh.devices.shape
    mesh = Mesh(
        mesh.devices.reshape(blocks // 8, 2, 2, 2, cores), ("h", "a", "y", "x", "mp")
    )
    blk = ("h", "a", "y", "x")
    placed = (
        P(blk, None),
        P(blk, None),
        P(),
        P(blk, "mp"),
        P("mp"),
        P(blk, "mp"),
        P("mp"),
        P(blk, "mp"),
        P("mp"),
        P("mp", blk),
        P(),
        P(blk, "mp"),
        P(blk, "mp"),
        P("mp", blk),
        P(),
        P(),
    )
    return jax.shard_map(
        shards,
        mesh=mesh,
        in_specs=placed,
        out_specs=(
            P(blk, None),
            P(blk, None),
            P(),
            P(blk, "mp"),
            P("mp"),
            P(blk, "mp"),
            P("mp"),
            P(blk, "mp"),
            P("mp"),
            P("mp", blk),
            P(),
            P(blk, "mp"),
            P(blk, "mp"),
            P("mp", blk),
        ),
        check_vma=False,
    )
```

```python
import functools

import jax
import jax.numpy as jnp
from jax import lax
from jax.experimental import pallas as pl
from jax.experimental.pallas import tpu as pltpu
from jax.sharding import Mesh
from jax.sharding import PartitionSpec as P

HD = 128
SEG = 1024
LOG2E = 1.4426950408889634
BIG = -1e30
BF = jnp.bfloat16
F32 = jnp.float32

epsilon = 1e-06


BLK = ("h", "a", "y", "x")
CUBE_AXES = ("a", "y", "x")


def bit_axis(bit):
    return ("x", "y", "a")[bit] if bit < 3 else "h", 1 if bit < 3 else 1 << (bit - 3)


def flip(value, bit):
    axis, mask = bit_axis(bit)
    return lax.ppermute(value, axis, [(i, i ^ mask) for i in range(lax.axis_size(axis))])


def mine(bit):
    axis, mask = bit_axis(bit)
    return (lax.axis_index(axis) // mask) % 2


def swap_mp(value):
    return lax.ppermute(value, "mp", [(0, 1), (1, 0)])


def halves(value, which):
    return lax.dynamic_index_in_dim(value, which, 0, keepdims=False)


def trade(value, axes, dim=0):
    return lax.all_to_all(value, axes, dim, dim, tiled=True)


def after(value, *others):
    if not others:
        return value
    return lax.optimization_barrier((value,) + others)[0]


def together(values):
    return list(lax.optimization_barrier(tuple(values)))


class Gather:
    def __init__(self, value):
        self.value, self.have = value, []

    def step(self, bit):
        at = sum(1 for b in self.have if b > bit)
        other = flip(self.value, bit)
        self.last = other
        self.value = jnp.where(
            mine(bit) == 0,
            jnp.stack([self.value, other], at),
            jnp.stack([other, self.value], at),
        )
        self.have.append(bit)
        return self

    def split(self, count):
        parts = []
        for value in jnp.split(self.value, count, axis=-1):
            part = Gather(value)
            part.have = list(self.have)
            parts.append(part)
        return parts

    def rows(self):
        return self.value.reshape((-1, self.value.shape[-1]))


class Scatter:
    def __init__(self, value, bits):
        self.have = list(range(bits))[::-1]
        self.value = value.reshape((2,) * bits + (-1, value.shape[-1]))

    def step(self, bit, *others):
        at = self.have.index(bit)
        me = mine(bit)
        keep = lax.dynamic_index_in_dim(self.value, me, at, keepdims=False)
        send = lax.dynamic_index_in_dim(self.value, 1 - me, at, keepdims=False)
        self.last = flip(send, bit)
        if others:
            self.last = after(self.last, *others)
        self.value = keep.astype(F32) + self.last.astype(F32)
        self.have.remove(bit)
        if self.have:
            self.value = self.value.astype(BF)
        return self


def joined(parts):
    one = Gather(jnp.concatenate([p.value for p in parts], axis=-1))
    one.have = list(parts[0].have)
    return one


CUBE = ((0, 1, 2), (1, 2, 0), (2, 0, 1))


def cube_parts(rows):
    units = rows // 16
    return [(units + 2 - i) // 3 * 16 for i in range(3)]


def cube_gather(value):
    parts, at = [], 0
    for size in cube_parts(value.shape[0]):
        parts.append(value[at : at + size])
        at += size
    for step in range(3):
        came = together([flip(part, order[step]) for part, order in zip(parts, CUBE)])
        parts = [jnp.concatenate(both, 0) for both in zip(parts, came)]
    return jnp.concatenate(parts, 0), came


class Cube:
    def __init__(self, value):
        self.value, self.size, self.have = value, value.shape[0], [0]

    def step(self, bit):
        self.last = flip(self.value, bit)
        self.value = jnp.concatenate([self.value, self.last], 0)
        self.have = self.have + [h ^ (1 << bit) for h in self.have]
        return self

    def done(self):
        pieces, at = [], 0
        for rows, order in zip(cube_parts(self.size), CUBE):
            wanted = [0]
            for bit in order:
                wanted = wanted + [w ^ (1 << bit) for w in wanted]
            pieces += [(self.have.index(w) * self.size + at, rows) for w in wanted]
            at += rows

        def kernel(value, out):
            place = 0
            for start, rows in pieces:
                out[place : place + rows] = value[start : start + rows]
                place += rows

        vmem = pl.BlockSpec(memory_space=pltpu.VMEM)
        return pl.pallas_call(
            kernel,
            out_shape=jax.ShapeDtypeStruct(self.value.shape, BF),
            in_specs=[vmem],
            out_specs=vmem,
            compiler_params=pltpu.CompilerParams(vmem_limit_bytes=16 * 2**20),
            cost_estimate=pl.CostEstimate(flops=0, bytes_accessed=2**23, transcendentals=0),
        )(self.value)


class CubeSum:
    def __init__(self, value, rows):
        self.parts, self.number, at = [], 0, 0
        for size in cube_parts(rows):
            self.parts.append(value[at : at + 8 * size])
            at += 8 * size

    def step(self, *others):
        half = [part.shape[0] // 2 for part in self.parts]
        sent = [
            flip(after(p[n:], *others), order[2 - self.number])
            for p, n, order in zip(self.parts, half, CUBE)
        ]
        self.came = together(sent)
        self.parts = [
            p[:n].astype(F32) + v.astype(F32) for p, n, v in zip(self.parts, half, self.came)
        ]
        self.number += 1
        if self.number < 3:
            self.parts = [p.astype(BF) for p in self.parts]
        return self

    def total(self):
        return jnp.concatenate(self.parts, 0)


def rotate(value, cosine, sine):
    half = value.shape[-1] // 2
    return value * cosine + jnp.concatenate([value[:, half:], value[:, :half]], axis=1) * sine


def rope_tables(position):
    freq = jnp.power(10000.0, -(jnp.arange(HD // 2, dtype=F32) * (2.0 / HD)))
    angle = position.astype(F32)[:, None] * freq[None, :]
    cosine, sine = jnp.cos(angle), jnp.sin(angle)
    return (jnp.concatenate([cosine, cosine], 1), jnp.concatenate([-sine, sine], 1))


def look(table, index):
    places = jnp.arange(table.shape[0], dtype=jnp.int32)
    return jnp.sum(jnp.where(index[:, None] == places[None, :], table[None, :], 0), axis=1)


def norm_back(grad, value, inverse, gain):
    scaled = grad * gain
    grad_gain = jnp.sum(grad * value * inverse, axis=0)
    mean_term = jnp.mean(scaled * value, axis=-1, keepdims=True)
    grad_value = inverse * scaled - value * (inverse * inverse * inverse) * mean_term
    return (grad_value, grad_gain)


NT = (((1,), (1,)), ((), ()))
TN = (((0,), (0,)), ((), ()))


def dot(left, right, dims=(((1,), (0,)), ((), ()))):
    return lax.dot_general(left, right, dims, preferred_element_type=F32)


def attend_kernel(vis, q_ref, kv_ref, o_ref, low_ref, lse_ref, acc, top, tot):
    rows, width = q_ref.shape
    heads = width // HD
    blocks = kv_ref.shape[0]
    factor = HD ** (-0.5) * LOG2E

    def block(place, first):
        key = kv_ref[place, :, :HD]
        value = kv_ref[place, :, HD:].astype(F32).T.astype(BF)
        if first:
            mask = lax.broadcasted_iota(jnp.int32, (rows, rows), 0) <= lax.broadcasted_iota(
                jnp.int32, (rows, rows), 1
            )
        for h in range(heads):
            scores = dot(key, q_ref[:, h * HD : (h + 1) * HD], NT) * factor
            if first:
                scores = jnp.where(mask, scores, BIG)
                best = jnp.max(scores, axis=0, keepdims=True)
                weights = jnp.exp2(scores - best)
                tot[h] = jnp.sum(weights, axis=0, keepdims=True)
                acc[h] = dot(value, weights.astype(BF))
            else:
                old = top[h]
                best = jnp.maximum(old, jnp.max(scores, axis=0, keepdims=True))
                weights = jnp.exp2(scores - best)
                scale = jnp.exp2(old - best)
                tot[h] = tot[h] * scale + jnp.sum(weights, axis=0, keepdims=True)
                acc[h] = acc[h] * scale + dot(value, weights.astype(BF))
            top[h] = best

    block(vis[blocks], True)

    def step(place, carry):
        @pl.when(vis[place] == 1)
        def _():
            block(place, False)

        return carry

    lax.fori_loop(0, blocks, step, 0)
    for h in range(heads):
        cols = slice(h * HD, (h + 1) * HD)
        total = tot[h]
        out = (acc[h] / total).T
        o_ref[:, cols] = out
        low_ref[:, cols] = out.astype(BF)
        lse_ref[h] = top[h] + jnp.log(total) * LOG2E


def attend(vis, query, keyval):
    rows, width = query.shape
    heads = width // HD
    smem = pl.BlockSpec(memory_space=pltpu.SMEM)
    vmem = pl.BlockSpec(memory_space=pltpu.VMEM)
    return pl.pallas_call(
        attend_kernel,
        out_shape=(
            jax.ShapeDtypeStruct((rows, width), F32),
            jax.ShapeDtypeStruct((rows, width), BF),
            jax.ShapeDtypeStruct((heads, 1, rows), F32),
        ),
        in_specs=[smem, vmem, vmem],
        out_specs=(vmem, vmem, vmem),
        scratch_shapes=[
            pltpu.VMEM((heads, HD, rows), F32),
            pltpu.VMEM((heads, 1, rows), F32),
            pltpu.VMEM((heads, 1, rows), F32),
        ],
        compiler_params=pltpu.CompilerParams(vmem_limit_bytes=40 * 2**20),
        cost_estimate=pl.CostEstimate(
            flops=4 * rows * width * 2048, bytes_accessed=8 * 2**20, transcendentals=rows * 6 * 2048
        ),
    )(vis, query, keyval)


def attend_back_kernel(
    vis, q_ref, kv_ref, do_ref, o_ref, lse_ref, cos_ref, sin_ref, out_ref, dkv_ref, dq_ref, delta
):
    rows, width = q_ref.shape
    heads = width // HD
    blocks = kv_ref.shape[0]
    scale = HD ** (-0.5)
    for h in range(heads):
        cols = slice(h * HD, (h + 1) * HD)
        product = (do_ref[:, cols].astype(F32) * o_ref[:, cols]).T
        delta[h] = jnp.sum(product, axis=0, keepdims=True)

    def block(place, first):
        key = kv_ref[place, :, :HD]
        value = kv_ref[place, :, HD:]
        if first:
            mask = lax.broadcasted_iota(jnp.int32, (rows, rows), 0) <= lax.broadcasted_iota(
                jnp.int32, (rows, rows), 1
            )
        dk = jnp.zeros((rows, HD), F32)
        dv = jnp.zeros((rows, HD), F32)
        for h in range(heads):
            cols = slice(h * HD, (h + 1) * HD)
            query = q_ref[:, cols]
            grad = do_ref[:, cols]
            probs = jnp.exp2(dot(key, query, NT) * (scale * LOG2E) - lse_ref[h])
            if first:
                probs = jnp.where(mask, probs, 0.0)
            dv = dv + dot(probs.astype(BF), grad)
            dprobs = dot(value, grad, NT)
            dscores = (probs * (dprobs - delta[h])).astype(BF)
            dk = dk + dot(dscores, query)
            dq = dot(dscores, key, TN)
            if first:
                dq_ref[:, cols] = dq
            else:
                dq_ref[:, cols] = dq_ref[:, cols] + dq
        dkv_ref[place, :, :HD] = (dk * scale).astype(BF)
        dkv_ref[place, :, HD:] = dv.astype(BF)

    block(vis[blocks], True)

    def step(place, carry):
        @pl.when(vis[place] == 1)
        def _():
            block(place, False)

        @pl.when((vis[place] == 0) & (place != vis[blocks]))
        def _():
            dkv_ref[place] = jnp.zeros((rows, 2 * HD), BF)

        return carry

    lax.fori_loop(0, blocks, step, 0)
    for h in range(heads):
        cols = slice(h * HD, (h + 1) * HD)
        out_ref[:, cols] = turn(dq_ref[:, cols] * scale, cos_ref[...], -sin_ref[...]).astype(BF)


def attend_back(vis, query, keyval, grad, out, lse, cosine, sine):
    rows, width = query.shape
    heads = width // HD
    smem = pl.BlockSpec(memory_space=pltpu.SMEM)
    vmem = pl.BlockSpec(memory_space=pltpu.VMEM)
    return pl.pallas_call(
        attend_back_kernel,
        out_shape=(
            jax.ShapeDtypeStruct((rows, width), BF),
            jax.ShapeDtypeStruct(keyval.shape, BF),
        ),
        in_specs=[smem] + [vmem] * 7,
        out_specs=(vmem, vmem),
        scratch_shapes=[
            pltpu.VMEM((rows, width), F32),
            pltpu.VMEM((heads, 1, rows), F32),
        ],
        compiler_params=pltpu.CompilerParams(vmem_limit_bytes=48 * 2**20),
        cost_estimate=pl.CostEstimate(
            flops=10 * rows * width * 2048,
            bytes_accessed=16 * 2**20,
            transcendentals=rows * 6 * 2048,
        ),
    )(vis, query, keyval, grad, out, lse, cosine, sine)


def turn(value, cosine, sine):
    return value * cosine + pltpu.roll(value, HD // 2, 1) * sine


def project_kernel(turned, x_ref, w_ref, b_ref, cos_ref, sin_ref, o_ref):
    lin = dot(x_ref[...], w_ref[...]) + b_ref[...]
    for h in range(lin.shape[1] // HD):
        cols = slice(h * HD, (h + 1) * HD)
        head = lin[:, cols]
        if h < turned:
            head = turn(head, cos_ref[...], sin_ref[...])
        o_ref[:, cols] = head.astype(BF)


def project(normed, weight, bias, cosine, sine, turned):
    rows = normed.shape[0]
    width = weight.shape[1]
    vmem = pl.BlockSpec(memory_space=pltpu.VMEM)
    return pl.pallas_call(
        functools.partial(project_kernel, turned),
        out_shape=jax.ShapeDtypeStruct((rows, width), BF),
        in_specs=[vmem] * 5,
        out_specs=vmem,
        compiler_params=pltpu.CompilerParams(vmem_limit_bytes=24 * 2**20),
        cost_estimate=pl.CostEstimate(
            flops=2 * rows * width * normed.shape[1],
            bytes_accessed=2 * normed.shape[1] * (rows + width),
            transcendentals=0,
        ),
    )(normed, weight, bias.astype(F32)[None], cosine, sine)


def share(tiles, chip):
    at = (chip * tiles) // 8
    return at, ((chip + 1) * tiles) // 8 - at


def pack_kernel(tiles, part, gate_ref, up_ref, down_ref, both_out, down_out):
    at, count = share(tiles, pl.program_id(0))
    cols = pl.ds(pl.multiple_of(at * 128, 128), part)
    keep = lax.broadcasted_iota(jnp.int32, (gate_ref.shape[0], part), 1) < count * 128

    def kept(value):
        return jnp.where(keep, value.astype(F32), 0.0).astype(BF)

    both_out[0, :, :part] = kept(gate_ref[:, cols])
    both_out[0, :, part:] = kept(up_ref[:, cols])
    down_out[0] = kept(down_ref[:, cols])


def pack(w_gate, w_up, w_down, part):
    slab, hidden = w_gate.shape
    vmem = pl.BlockSpec(memory_space=pltpu.VMEM)
    return pl.pallas_call(
        functools.partial(pack_kernel, hidden // 128, part),
        grid=(8,),
        out_shape=(
            jax.ShapeDtypeStruct((8, slab, 2 * part), BF),
            jax.ShapeDtypeStruct((8, slab, part), BF),
        ),
        in_specs=[vmem] * 3,
        out_specs=(
            pl.BlockSpec((1, slab, 2 * part), lambda c: (c, 0, 0)),
            pl.BlockSpec((1, slab, part), lambda c: (c, 0, 0)),
        ),
        compiler_params=pltpu.CompilerParams(vmem_limit_bytes=24 * 2**20),
        cost_estimate=pl.CostEstimate(flops=0, bytes_accessed=8 * 2**20, transcendentals=0),
    )(w_gate, w_up, w_down)


def unpack_kernel(tiles, gate_ref, up_ref, down_ref, gate_out, up_out, down_out):
    for c in range(8):
        at, size = share(tiles, c)
        here, width = slice(at * 128, (at + size) * 128), size * 128
        gate_out[:, here] = gate_ref[c, :, :width].astype(F32)
        up_out[:, here] = up_ref[c, :, :width].astype(F32)
        down_out[:, here] = down_ref[c, :, :width].astype(F32)


def unpack(gate, up, down, hidden):
    slab = down.shape[1]
    vmem = pl.BlockSpec(memory_space=pltpu.VMEM)
    return pl.pallas_call(
        functools.partial(unpack_kernel, hidden // 128),
        out_shape=(
            jax.ShapeDtypeStruct((slab, hidden), F32),
            jax.ShapeDtypeStruct((slab, hidden), F32),
            jax.ShapeDtypeStruct((slab, hidden), F32),
        ),
        in_specs=[vmem] * 3,
        out_specs=(vmem,) * 3,
        compiler_params=pltpu.CompilerParams(vmem_limit_bytes=40 * 2**20),
        cost_estimate=pl.CostEstimate(flops=0, bytes_accessed=10 * 2**20, transcendentals=0),
    )(gate, up, down)


def shards(
    tokens,
    cotangent,
    norm_gain,
    w_query,
    b_query,
    w_key,
    b_key,
    w_value,
    b_value,
    w_out,
    ffn_gain,
    w_gate,
    w_up,
    w_down,
    unit_seq,
    block_map,
):
    rows, model = tokens.shape
    blocks = block_map.shape[0]
    low_rows = rows // 2
    width = w_query.shape[1]
    heads = width // HD
    slab = w_gate.shape[0]
    tiles = w_gate.shape[1] // 128
    part = -(-tiles // 8) * 128
    core = lax.axis_index("mp")
    me = lax.axis_index(BLK)

    def my_half(value):
        return halves(value.reshape((2, low_rows) + value.shape[1:]), core)

    def whole(own):
        other = swap_mp(own)
        return jnp.where(
            core == 0, jnp.concatenate([own, other], 0), jnp.concatenate([other, own], 0)
        )

    bits = blocks.bit_length() - 1
    high = list(range(3, bits))[::-1]

    both_send, down_send = pack(w_gate, w_up, w_down.T, part)
    w_kv = Gather(jnp.concatenate([w_key, w_value], axis=1))
    w_q = Gather(w_query)
    w_out_all = Gather(w_out.T)
    cot_half = my_half(cotangent)
    cot_cube = Cube(cot_half)
    for bit in high:
        w_kv.step(bit)
        w_q.step(bit)
        w_out_all.step(bit)
    cot_cube.step(2)
    near = [after(my_half(tokens), w_kv.last)]
    for bit in high[::-1]:
        near = near + [flip(v, bit) for v in near]
    both_cube = trade(after(both_send, w_kv.last), CUBE_AXES)
    down_near = [after(down_send, w_kv.last)]
    for bit in high[::-1]:
        down_near = down_near + [flip(v, bit) for v in down_near]
    both_own = lax.all_gather(both_cube.reshape(8 * slab, -1), "h", axis=0, tiled=True)
    block_map = after(block_map, both_send)
    inputs = after(tokens, both_send).astype(F32)
    per_unit = SEG // rows
    units = jnp.arange(unit_seq.shape[0], dtype=jnp.int32)
    previous = jnp.concatenate([jnp.full((1,), -1, jnp.int32), unit_seq[:-1]])
    first_unit = lax.cummax(jnp.where(unit_seq != previous, units, 0), axis=0)
    seqs = look(unit_seq, block_map // per_unit)
    own_place = jnp.arange(blocks, dtype=jnp.int32) == me
    my_block = jnp.sum(jnp.where(own_place, block_map, 0))
    my_seq = jnp.sum(jnp.where(own_place, seqs, 0))
    vis = ((seqs == my_seq) & (block_map < my_block)).astype(jnp.int32)
    vis = jnp.concatenate([vis, me[None].astype(jnp.int32)])
    places = jnp.bitwise_xor(me, 8 * jnp.arange(blocks // 8, dtype=jnp.int32))
    near_blocks = look(block_map, places)
    begin = look(first_unit, near_blocks // per_unit)
    position = (near_blocks * rows - begin * SEG)[:, None] + jnp.arange(rows, dtype=jnp.int32)
    cosine_all, sine_all = rope_tables(position.reshape(-1))
    cosine, sine = cosine_all[:rows], sine_all[:rows]

    gain_one = norm_gain.astype(F32)

    def norm_one(value):
        inverse = lax.rsqrt(jnp.mean(value * value, axis=-1, keepdims=True) + epsilon)
        return inverse, (value * inverse * gain_one).astype(BF)

    inverse_one, normed = norm_one(inputs)
    normed_near = [norm_one(after(whole(v), both_send).astype(F32))[1] for v in near[1:]]
    normed_near = jnp.concatenate([normed] + normed_near, 0)
    w_kv.value = after(w_kv.value, both_cube, cosine, vis, normed_near)
    w_q.value = after(w_q.value, both_cube)
    w_kv.step(2)
    w_q.step(2)
    one, two = w_q.split(2)
    w_kv.step(1)
    one.step(0)
    two.step(1)
    w_out_all.value = after(w_out_all.value, w_q.last)
    w_out_all.step(2)
    w_kv = w_kv.step(0).rows()
    w_q = joined([one.step(1), two.step(0)]).rows()
    q_last = (one.last, two.last)

    keyval = project(
        normed_near, w_kv, jnp.concatenate([b_key, b_value]), cosine_all, sine_all, 1
    )
    keyval = list(keyval.reshape(blocks // 8, rows, 2 * HD))
    for bit in high:
        mask = 1 << (bit - 3)
        keyval = [jnp.where(mine(bit) == 0, v, keyval[k ^ mask]) for k, v in enumerate(keyval)]
    keyval = Gather(jnp.stack(keyval, 0).reshape((2,) * len(high) + (rows, 2 * HD)))
    keyval.have = list(high)
    keyval.value = after(keyval.value, w_out_all.last)
    w_out_all.value = after(w_out_all.value, w_kv)
    cot_cube.value = after(cot_cube.value, w_kv)
    keyval.step(2)
    w_out_all.step(0)
    cot_cube.step(1)
    key_part, value_part = keyval.split(2)
    key_part.value = after(key_part.value, w_out_all.last, cot_cube.last, *q_last)
    key_part.step(0)
    value_part.step(1)
    key_part.step(1)
    value_part.step(0)
    for bit in high:
        mask = 1 << (bit - 3)
        down_near = [
            jnp.where(mine(bit) == 0, v, down_near[k ^ mask]) for k, v in enumerate(down_near)
        ]
    down_near = after(jnp.stack(down_near, 0), key_part.last, value_part.last)
    down_own = trade(down_near, CUBE_AXES, 1).reshape(model, part)
    w_out_all.value = after(w_out_all.value, key_part.last, value_part.last)
    cot_cube.value = after(cot_cube.value, key_part.last, value_part.last)
    keyval = joined([key_part, value_part]).value.reshape(blocks, rows, 2 * HD)
    out_full = w_out_all.step(1).rows()
    cot_cube.step(0)
    query = project(normed, w_q, b_query, cosine, sine, heads)
    attended, attended_low, lse = attend(vis, query, keyval)
    attended_low = after(attended_low, cot_cube.last, down_own, both_own)
    cot_cube = cot_cube.done()
    attn = dot(attended_low, out_full, NT).astype(BF).reshape(2, low_rows, model)
    attn = halves(attn, core).astype(F32) + swap_mp(halves(attn, 1 - core)).astype(F32)
    middle = my_half(tokens).astype(F32) + attn
    gain_two = ffn_gain.astype(F32)
    inverse_two = lax.rsqrt(jnp.mean(middle * middle, axis=-1, keepdims=True) + epsilon)
    normed_two = (middle * inverse_two * gain_two).astype(BF)
    cube_two, came = cube_gather(normed_two)
    both_w = (both_own, swap_mp(both_own))
    down_w = (down_own, swap_mp(down_own))

    def over_high_back(value):
        return lax.psum_scatter(value, "h", scatter_dimension=0, tiled=True)

    lins, hiddens, grads = [], [], []
    for both in both_w:
        lin = dot(cube_two, both)
        gate, up = lin[:, :part], lin[:, part:]
        sigmoid_gate = jax.nn.sigmoid(gate)
        silu_gate = gate * sigmoid_gate
        hiddens.append((silu_gate * up).astype(BF))
        lins.append((gate, up, sigmoid_gate, silu_gate))
    for (gate, up, sigmoid_gate, silu_gate), down in zip(lins, down_w):
        grad_hidden = dot(cot_cube, down)
        grad_gate = grad_hidden * up * sigmoid_gate * (1.0 + gate * (1.0 - sigmoid_gate))
        grad_up = grad_hidden * silu_gate
        grads.append(jnp.concatenate([grad_gate.astype(BF), grad_up.astype(BF)], axis=1))
    grad_two = dot(grads[0], both_w[0], NT) + dot(grads[1], both_w[1], NT)
    grad_two = grad_two.astype(BF)
    grads = [after(v, grad_two) for v in grads]
    hiddens = [after(v, grad_two) for v in hiddens]
    grad_two = CubeSum(grad_two, low_rows).step()
    gates, ups = [g[:, :part] for g in grads], [g[:, part:] for g in grads]
    theirs = [
        dot(cot_cube, hiddens[1], TN).astype(BF),
        dot(cube_two, gates[1], TN).astype(BF),
        dot(cube_two, ups[1], TN).astype(BF),
    ]
    came = [swap_mp(v) for v in theirs]
    grad_two.step(*theirs)
    down_back = (dot(cot_cube, hiddens[0], TN) + came[0].astype(F32)).astype(BF)
    down_high = over_high_back(down_back)
    gate_back = (dot(cube_two, gates[0], TN) + came[1].astype(F32)).astype(BF)
    gate_high = over_high_back(gate_back)
    grad_two.step(down_back, gate_back)
    up_back = (dot(cube_two, ups[0], TN) + came[2].astype(F32)).astype(BF)
    up_high = over_high_back(up_back)
    grad_two = after(grad_two.total(), up_back)

    grad_middle_norm, grad_gain_two = norm_back(grad_two, middle, inverse_two, gain_two)
    grad_middle_half = cot_half.astype(F32) + grad_middle_norm
    grad_attn = whole(grad_middle_half.astype(BF))
    grad_middle = whole(grad_middle_half)
    grad_attended = dot(grad_attn, out_full).astype(BF)
    out_grad = dot(grad_attn, attended_low, TN).astype(BF)
    grad_q, grad_kv_all = attend_back(
        vis, query, keyval, grad_attended, attended, lse, cosine, sine
    )
    low = [2] + high[::-1]

    def pair(grad):
        n = grad.shape[1] // 2
        return [Scatter(grad[:, :n], bits), Scatter(grad[:, n:], bits)]

    def merge(parts):
        parts[0].value = jnp.concatenate([p.value for p in parts], axis=-1)
        return parts[0]

    def hold(parts, *others):
        for p in parts:
            p.value = after(p.value, *others)

    def home(value, *others):
        return trade(after(value, *others).reshape(8, slab, part), CUBE_AXES)

    out_sum = pair(out_grad)
    out_sum[0].step(0)
    out_sum[1].step(1)
    kv_sum = pair(grad_kv_all.reshape(blocks * rows, 2 * HD))
    hold(kv_sum, out_sum[0].last, out_sum[1].last)
    kv_sum[0].step(0)
    kv_sum[1].step(1)
    hiddens = [after(v, kv_sum[0].last) for v in hiddens]
    ffn = (dot(hiddens[0], down_w[0], NT) + dot(hiddens[1], down_w[1], NT)).astype(BF)
    query_grad = dot(normed, after(grad_q, kv_sum[0].last), TN).astype(BF)
    kv_sum[0].step(1)
    kv_sum[1].step(0)
    hold(out_sum, kv_sum[0].last, kv_sum[1].last)
    kv_sum = merge(kv_sum)
    kv_sum.step(2)
    hold(out_sum, kv_sum.last)
    query_sum = pair(query_grad)
    hold(query_sum, kv_sum.last)
    out_sum[0].step(1)
    out_sum[1].step(0)
    query_sum[0].step(0)
    query_sum[1].step(1)
    down_back = home(down_high, kv_sum.last)
    ffn = CubeSum(ffn, low_rows)
    for bit in high[::-1]:
        kv_sum.step(bit)
    out_sum = merge(out_sum)
    hold([out_sum], kv_sum.last)
    grad_k = rotate(kv_sum.value[:, :HD], cosine, -sine).astype(BF)
    grad_v = kv_sum.value[:, HD:].astype(BF)
    grad_kv = jnp.concatenate([grad_k, grad_v], axis=1)
    last = Scatter(dot(normed, grad_kv, TN).astype(BF), bits)
    last.step(1)
    grad_normed = (dot(grad_q, w_q, NT) + dot(grad_kv, w_kv, NT)).astype(BF)
    other_normed = swap_mp(grad_normed)
    hold([last], other_normed, query_sum[0].last, query_sum[1].last)
    last.step(0)
    hold([out_sum], last.last)
    hold(query_sum, last.last)
    query_sum[0].step(1)
    query_sum[1].step(0)
    query_sum = merge(query_sum)
    last.step(2)
    hold([out_sum], last.last)
    hold([query_sum], last.last)
    for bit in high[::-1]:
        last.step(bit)
    gate_back = home(gate_high, down_back, last.last)
    out_sum.step(2)
    query_sum.step(2)
    grad_normed = grad_normed.astype(F32) + other_normed.astype(F32)
    grad_input_norm, grad_gain_one = norm_back(grad_normed, inputs, inverse_one, gain_one)
    grad_tokens = grad_middle + grad_input_norm
    bias_query = jnp.sum(grad_q.astype(F32), axis=0)
    bias_kv = jnp.sum(grad_kv.astype(F32), axis=0)
    gain_two_sum = grad_gain_two + swap_mp(grad_gain_two)
    small = jnp.concatenate([grad_gain_one, gain_two_sum, bias_query, bias_kv]).reshape(-1, 128)
    came = flip(after(small, last.last), 0)
    small = small + came
    hold([out_sum], query_sum.last, came)
    hold([query_sum], out_sum.last, came)
    ffn.step(last.last)
    for bit in high[::-1]:
        out_sum.step(bit)
        query_sum.step(bit)
    came = flip(after(small, out_sum.last, query_sum.last), 1)
    small = small + came
    up_back = home(up_high, gate_back, *ffn.came)
    ffn.step(came)
    small = small + flip(after(small, *ffn.came), 2)
    for bit in high:
        small = small + flip(small, bit)
    ffn.step()
    mixed = whole((middle + ffn.total()).astype(BF))
    small = small.reshape(-1)
    out_part, query_part, kv_part = out_sum.value, query_sum.value, last.value

    gate_part, up_part, down_part = unpack(gate_back, up_back, down_back, w_gate.shape[1])
    gain_one_sum = small[:model]
    gain_two_sum = small[model : 2 * model]
    bias_query_sum = small[2 * model : 2 * model + width]
    bias_key_sum = small[2 * model + width : 2 * model + width + HD]
    bias_value_sum = small[2 * model + width + HD :]
    return (
        mixed,
        grad_tokens,
        gain_one_sum,
        query_part,
        bias_query_sum,
        kv_part[:, :HD],
        bias_key_sum,
        kv_part[:, HD:],
        bias_value_sum,
        out_part.T,
        gain_two_sum,
        gate_part,
        up_part,
        down_part.T,
    )


def solution(mesh):
    blocks, cores = mesh.devices.shape
    mesh = Mesh(
        mesh.devices.reshape(blocks // 8, 2, 2, 2, cores), ("h", "a", "y", "x", "mp")
    )
    blk = ("h", "a", "y", "x")
    placed = (
        P(blk, None),
        P(blk, None),
        P(),
        P(blk, "mp"),
        P("mp"),
        P(blk, "mp"),
        P("mp"),
        P(blk, "mp"),
        P("mp"),
        P("mp", blk),
        P(),
        P(blk, "mp"),
        P(blk, "mp"),
        P("mp", blk),
        P(),
        P(),
    )
    return jax.shard_map(
        shards,
        mesh=mesh,
        in_specs=placed,
        out_specs=(
            P(blk, None),
            P(blk, None),
            P(),
            P(blk, "mp"),
            P("mp"),
            P(blk, "mp"),
            P("mp"),
            P(blk, "mp"),
            P("mp"),
            P("mp", blk),
            P(),
            P(blk, "mp"),
            P(blk, "mp"),
            P("mp", blk),
        ),
        check_vma=False,
    )
```
